256 devices in a mesh: segment: 4 (over y), rows: 64 (over z, x, core).
Axes of the slice: x: 4, y: 4, z: 8, core: 2. Of those that a mesh axis runs over, the one named last changes fastest.
Arguments:
- state: bfloat16 [4, 2, 128, 23040], P('segment', None, 'rows'), may hold values from -6 to 6
- bounds: int32 [5], replicated, may hold values from 0 to 5, as said below
- timesteps: int32 [2], replicated, may hold values from 0 to 999
- gains: float32 [4, 2, 320], P('segment'), may hold values from 0.1 to 1.9
- spatial_weight: bfloat16 [4, 2, 3, 3, 320, 320], P('segment'), may hold values from -0.109375 to 0.109375
- temporal_weight: bfloat16 [4, 2, 3, 320, 320], P('segment'), may hold values from -0.1875 to 0.1875
- time_weight: float32 [4, 2, 320, 320], P('segment'), may hold values from -0.5 to 0.5
Outputs:
- new_state: bfloat16 [4, 2, 128, 23040], P('segment', None, 'rows')
The draws below stay inside these ranges and needn't reach their ends.
Inputs may be any that keep to these rules, and one draw needn't show every extreme that they name: bounds[0] = 0, bounds[4] = 5, and every component holds 1 or 2 blocks; slot 1 of a component with one block may be computed but is not kept.
All inputs are finite; a program needn't handle non-finite values.
Results may differ from the reference program's by a relative error of at most 0.0065.
Values may be sent and summed in bfloat16 or wider, within the bound.
A program may use at most 64 MiB of HBM per device.

```python
import math
import jax
import jax.numpy as jnp
from jax import lax

C = 320
TEMB = 320
W = 72
FRAMES = 2
STEPS = 2
H = 128
N_SEGMENT = 4


def draw_bounds(key, part):
    key = jax.random.fold_in(key, 7)
    extra = jax.random.randint(key, (), 0, N_SEGMENT)
    counts = 1 + (jnp.arange(N_SEGMENT) == extra).astype(jnp.int32)
    return jnp.concatenate([jnp.zeros((1,), jnp.int32), jnp.cumsum(counts).astype(jnp.int32)])


def levels(stream_key, extent, shards, least, largest):
    level, own = 1.0, jax.random.fold_in(stream_key, 6)
    for position, shards_of in shards:
        heights = jnp.exp(jax.random.uniform(jax.random.fold_in(own, position), (shards_of,), jnp.float32, least / len(shards), largest / len(shards)))
        level = level * jnp.repeat(heights, extent[position] // shards_of).reshape([-1 if axis == position else 1 for axis in range(len(extent))])
    return level


def noise(key, extent, spread, limit, split=(), kind=jnp.bfloat16):
    entries = jax.random.normal(key, extent, jnp.float32) * spread
    if len(split) > 0:
        entries = levels(key, extent, split, -0.22, 0.18) * entries
    return jnp.clip(entries, min=-limit, max=limit).astype(kind)


def setup_inputs(seed: int = 0) -> dict:
    streams_of = jax.random.split(jax.random.key(seed), 8)
    state = noise(streams_of[0], (N_SEGMENT, FRAMES, H, W * C), 1.0, 6.0, ((0, 4), (2, 64)))
    bounds = draw_bounds(jax.random.fold_in(streams_of[7], 71), 0)
    timesteps = jax.random.randint(streams_of[2], (STEPS,), 0, 1000).astype(jnp.int32)
    gains = jnp.clip(1.0 + 0.18 * jax.random.normal(streams_of[3], (N_SEGMENT, 2, C), jnp.float32), 0.1, 1.9)
    spatial_weight = noise(streams_of[4], (N_SEGMENT, 2, 3, 3, C, C), (9 * C) ** -0.5, 0.109375, ((0, 4),))
    temporal_weight = noise(streams_of[5], (N_SEGMENT, 2, 3, C, C), (3 * C) ** -0.5, 0.1875, ((0, 4),))
    time_weight = noise(streams_of[6], (N_SEGMENT, 2, TEMB, C), (TEMB // 2) ** -0.5, 0.5, ((0, 4),), jnp.float32)
    return dict(state=state, bounds=bounds, timesteps=timesteps, gains=gains, spatial_weight=spatial_weight, temporal_weight=temporal_weight, time_weight=time_weight)


def embed(step_time):
    half = TEMB // 2
    freq = jnp.exp(-math.log(10000.0) * jnp.arange(half, dtype=jnp.float32) / half)
    angle = step_time.astype(jnp.float32) * freq
    return jnp.concatenate([jnp.cos(angle), jnp.sin(angle)])

def block_rows(extended, gain, spatial, temporal, bias):
    values = extended.astype(jnp.float32)
    scale = lax.rsqrt(lax.optimization_barrier(jnp.mean(values * values, axis=-1, keepdims=True)) + 1e-06)
    normed = (values * scale * gain).astype(jnp.bfloat16)
    padded = jnp.pad(normed, ((0, 0), (0, 0), (1, 1), (0, 0)))
    frames, rows_in, width, chans = extended.shape
    rows_out = rows_in - 2
    total = jnp.zeros((frames * rows_out * width, chans), jnp.float32) + bias
    for shift_y in range(3):
        for shift_x in range(3):
            window = padded[:, shift_y:shift_y + rows_out, shift_x:shift_x + width, :].reshape(-1, chans)
            total = total + jnp.dot(window, spatial[shift_y, shift_x], preferred_element_type=jnp.float32)
    activated = jax.nn.silu(total).astype(jnp.bfloat16).reshape(frames, rows_out, width, chans)
    framed = jnp.pad(activated, ((1, 1), (0, 0), (0, 0), (0, 0)))
    mixed = jnp.zeros_like(total)
    for tap in range(3):
        mixed = mixed + jnp.dot(framed[tap:tap + frames].reshape(-1, chans), temporal[tap], preferred_element_type=jnp.float32)
    center = extended[:, 1:-1].astype(jnp.float32).reshape(-1, chans)
    return (center + total + mixed).astype(jnp.bfloat16).reshape(frames, rows_out, width, chans)

def reference(state, bounds, timesteps, gains, spatial_weight, temporal_weight, time_weight):
    fields = state.reshape(N_SEGMENT, FRAMES, H, W, C)
    for step in range(STEPS):
        emb = embed(timesteps[step])
        bias_all = jnp.einsum('t,kjtc->kjc', emb, time_weight, precision=lax.Precision.HIGHEST)
        outputs = []
        for segment in range(N_SEGMENT):
            count = bounds[segment + 1] - bounds[segment]

            def apply(slot, field):
                extended = jnp.pad(field, ((0, 0), (1, 1), (0, 0), (0, 0)))
                return block_rows(extended, gains[segment, slot], spatial_weight[segment, slot], temporal_weight[segment, slot], bias_all[segment, slot])
            field = apply(0, fields[(segment - 1) % N_SEGMENT])
            second = apply(1, field)
            field = jnp.where(count > 1, second, field)
            outputs.append(field)
        fields = jnp.stack(outputs)
    return fields.reshape(N_SEGMENT, FRAMES, H, W * C)
```

```python
import math

import jax
import jax.numpy as jnp
from jax import lax
from jax.experimental import pallas as pl
from jax.experimental.pallas import tpu as pltpu
from jax.sharding import PartitionSpec as P

C = 320
W = 72
STEPS = 2
FRAMES = 2
SEGMENTS = 4
GROUPS = 64
MAIN = 256
REST = C - MAIN
PIX = FRAMES * W
PACK = 2 * MAIN + 2 * REST
NOUT = 4 * MAIN
MESH = pl.DeviceIdType.MESH
F32 = jnp.float32
BF16 = jnp.bfloat16


def lanes(shape):
    return lax.broadcasted_iota(jnp.int32, shape, len(shape) - 1)


def roll_rest(value):
    return pltpu.roll(value, REST, 1)


def norm_pair(pair, gain_main, gain_rest, xm, xr, at):
    main_a = pair[:, :MAIN].astype(F32)
    main_b = pair[:, MAIN : 2 * MAIN].astype(F32)
    rest = pair[:, 2 * MAIN :].astype(F32)
    low = lanes(rest.shape) < REST
    square = rest * rest
    zero = jnp.zeros_like(square)

    def scale(main, own):
        both = main * main
        total = both[:, :128] + both[:, 128:] + own
        return lax.rsqrt(jnp.sum(total, axis=-1, keepdims=True) * (1.0 / C) + 1e-06)

    scale_a = scale(main_a, jnp.where(low, square, zero))
    scale_b = scale(main_b, jnp.where(low, zero, square))
    xm[2 * at] = (main_a * scale_a * gain_main).astype(BF16)
    xm[2 * at + 1] = (main_b * scale_b * gain_main).astype(BF16)
    xr[at] = (rest * jnp.where(low, scale_a, scale_b) * gain_rest).astype(BF16)


def block(xm, xr, at, pair_a, pair_b, wm, wr, wt, slot, bias_main, bias_rest):
    left = jnp.concatenate([xm[pl.ds(2 * at + dy, 2)].reshape(2 * PIX, MAIN) for dy in range(3)], axis=1)
    left_rest = jnp.concatenate([xr[at], xr[at + 1]], axis=1)
    spot = lax.rem(lax.broadcasted_iota(jnp.int32, (2 * PIX, 1), 0), W)
    first, last = spot == 0, spot == W - 1

    def product(tile):
        cols = slice(tile * MAIN, (tile + 1) * MAIN)
        main = jnp.dot(left, wm[slot, :, cols], preferred_element_type=F32)
        rest = [jnp.dot(left_rest, wr[slot, row, :, cols], preferred_element_type=F32) for row in range(2)]
        return main + jnp.concatenate(rest, axis=0)

    def from_before(value):
        return jnp.where(first, 0.0, pltpu.roll(value, 1, 0))

    def from_after(value):
        return jnp.where(last, 0.0, pltpu.roll(value, value.shape[0] - 1, 0))

    a_main = from_before(product(0)) + product(1) + from_after(product(2)) + bias_main
    z = product(3)
    sides = from_before(z[:, :128]) + from_after(z[:, 128:])
    centre = z[:, :128]
    low = lanes((PIX, 128)) < REST
    a_rest = jnp.where(
        low,
        sides[:PIX] + roll_rest(centre[:PIX]),
        roll_rest(sides[PIX:]) + centre[PIX:],
    ) + bias_rest

    def silu(value):
        return value * (0.5 * jnp.tanh(0.5 * value) + 0.5)

    u_main = silu(a_main)
    u_rest = silu(a_rest)
    low = lanes((W, 128)) < REST

    def transposed(first_half, second_half):
        return (
            jnp.where(low, first_half, roll_rest(second_half)),
            jnp.where(low, roll_rest(first_half), second_half),
        )

    rest_a, rest_b = transposed(u_rest[:W], u_rest[W:])
    mixed = jnp.concatenate(
        [
            jnp.concatenate([u_main[:W], u_main[PIX : PIX + W]], axis=0),
            jnp.concatenate([u_main[W:PIX], u_main[PIX + W :]], axis=0),
            jnp.concatenate([rest_a, rest_b], axis=0),
        ],
        axis=1,
    ).astype(BF16)
    v = jnp.dot(mixed, wt[slot], preferred_element_type=F32)
    v_a = jnp.concatenate([v[:W, :MAIN], v[:W, MAIN : 2 * MAIN]], axis=0)
    v_b = jnp.concatenate([v[W:, :MAIN], v[W:, MAIN : 2 * MAIN]], axis=0)
    v_rest = jnp.concatenate(transposed(v[:W, 2 * MAIN :], v[W:, 2 * MAIN :]), axis=0)
    low = lanes((PIX, 128)) < REST
    h_a = pair_a[:, MAIN : 2 * MAIN].astype(F32)
    h_b = pair_b[:, :MAIN].astype(F32)
    h_rest = roll_rest(jnp.where(low, pair_b[:, 2 * MAIN :].astype(F32), pair_a[:, 2 * MAIN :].astype(F32)))
    return h_a + a_main[:PIX] + v_a, h_b + a_main[PIX:] + v_b, h_rest + a_rest + v_rest


def kernel(
    state, bounds, timesteps, gains, spatial, temporal, time_weight,
    out,
    raw_s, raw_t, raw_b, wm, wr, wt, packed, arrived, hidden, xm, xr, hm, hr,
    load_sem, send_sem, recv_sem,
):
    segment = lax.axis_index("segment")
    group = lax.axis_index("rows")
    core = lax.rem(group, 2)
    behind, ahead = lax.rem(segment + SEGMENTS - 1, SEGMENTS), lax.rem(segment + 1, SEGMENTS)
    across = group - 1 + 2 * core
    inner = group + 1 - 2 * core
    has_across = (across >= 0) & (across < GROUPS)

    loads = []
    for slot in range(2):
        loads.append(
            (
                pltpu.make_async_copy(spatial.at[slot], raw_s.at[slot], load_sem.at[slot, 0]),
                pltpu.make_async_copy(temporal.at[slot], raw_t.at[slot], load_sem.at[slot, 1]),
                pltpu.make_async_copy(time_weight.at[slot], raw_b.at[slot], load_sem.at[slot, 2]),
            )
        )
        for load in loads[-1]:
            load.start()

    barrier = pltpu.get_barrier_semaphore()
    pl.semaphore_signal(barrier, inc=1, device_id=(behind, group), device_id_type=MESH)
    pl.semaphore_signal(barrier, inc=1, device_id=(segment, inner), device_id_type=MESH)

    @pl.when(has_across)
    def _():
        pl.semaphore_signal(barrier, inc=1, device_id=(behind, across), device_id_type=MESH)

    rows = [[state[f, row].astype(F32) for f in range(FRAMES)] for row in range(2)]
    main = [jnp.concatenate([x[:, :MAIN] for x in row], axis=0) for row in rows]
    rest = [jnp.concatenate([x[:, MAIN:] for x in row], axis=0) for row in rows]
    packed[0] = jnp.concatenate(main + rest, axis=1).astype(BF16)

    pl.semaphore_wait(barrier, 2 + has_across.astype(jnp.int32))

    def own_copy(step):
        return pltpu.make_async_remote_copy(
            packed.at[step], arrived.at[step, 1], send_sem.at[step, 0], recv_sem.at[step, 0],
            device_id=(ahead, group), device_id_type=MESH,
        )

    def across_copy(step):
        return pltpu.make_async_remote_copy(
            packed.at[step], arrived.at[step, 2 - 2 * core], send_sem.at[step, 1], recv_sem.at[step, 1],
            device_id=(ahead, across), device_id_type=MESH,
        )

    def inner_copy(step):
        return pltpu.make_async_remote_copy(
            arrived.at[step, 1], arrived.at[step, 2 * core], send_sem.at[step, 2], recv_sem.at[step, 2],
            device_id=(segment, inner), device_id_type=MESH,
        )

    def send(step):
        own_copy(step).start()

        @pl.when(has_across)
        def _():
            across_copy(step).start()

    send(0)

    for slot in range(2):
        for load in loads[slot]:
            load.wait()
        for dy in range(3):
            for dx in range(3):
                wm[slot, dy * MAIN : (dy + 1) * MAIN, dx * MAIN : (dx + 1) * MAIN] = raw_s[slot, 3 * dy + dx, :MAIN, :MAIN]
                for row in range(2):
                    at = (dy + row) * REST
                    wr[slot, row, at : at + REST, dx * MAIN : (dx + 1) * MAIN] = raw_s[slot, 3 * dy + dx, MAIN:, :MAIN]
            rests = [raw_s[slot, 3 * dy + dx, :, MAIN:] for dx in range(3)]
            rests = jnp.concatenate(rests + [jnp.zeros_like(rests[0])], axis=1)
            wm[slot, dy * MAIN : (dy + 1) * MAIN, 3 * MAIN :] = rests[:MAIN]
            for row in range(2):
                at = (dy + row) * REST
                wr[slot, row, at : at + REST, 3 * MAIN :] = rests[MAIN:]
        wr[slot, 0, 3 * REST :] = jnp.zeros((REST, NOUT), BF16)
        wr[slot, 1, :REST] = jnp.zeros((REST, NOUT), BF16)
        for f in range(FRAMES):
            for g in range(FRAMES):
                tap = f - g + 1
                wt[slot, f * MAIN : (f + 1) * MAIN, g * MAIN : (g + 1) * MAIN] = raw_t[slot, tap, :MAIN, :MAIN]
                at = 2 * MAIN + f * REST
                wt[slot, at : at + REST, g * MAIN : (g + 1) * MAIN] = raw_t[slot, tap, MAIN:, :MAIN]
            rests = jnp.concatenate([raw_t[slot, f - g + 1, :, MAIN:] for g in range(FRAMES)], axis=1)
            wt[slot, f * MAIN : (f + 1) * MAIN, 2 * MAIN :] = rests[:MAIN]
            at = 2 * MAIN + f * REST
            wt[slot, at : at + REST, 2 * MAIN :] = rests[MAIN:]

    half = C // 2
    number = lax.broadcasted_iota(jnp.int32, (8, half), 1).astype(F32)
    which = lax.broadcasted_iota(jnp.int32, (8, half), 0)
    t = jnp.where(which == 0, timesteps[0], timesteps[1]).astype(F32)
    angle = t * jnp.exp(-math.log(10000.0) * number / half)
    emb = jnp.concatenate([jnp.cos(angle), jnp.sin(angle)], axis=1)
    bias = [
        jnp.dot(emb, raw_b[slot], preferred_element_type=F32, precision=lax.Precision.HIGHEST) for slot in range(2)
    ]

    def twice(value):
        return jnp.concatenate([value, value], axis=1)

    gain_main = [gains[slot : slot + 1, :MAIN] for slot in range(2)]
    gain_rest = [twice(gains[slot : slot + 1, MAIN:]) for slot in range(2)]
    two = jnp.full((1, 128), bounds[segment + 1] - bounds[segment], jnp.int32) > 1
    two_main = jnp.concatenate([two, two], axis=1)

    for step in range(STEPS):
        bias_main = [bias[slot][step : step + 1, :MAIN] for slot in range(2)]
        bias_rest = [twice(bias[slot][step : step + 1, MAIN:]) for slot in range(2)]

        def norm(at, step=step):
            norm_pair(arrived[step, at], gain_main[0], gain_rest[0], xm, xr, at)

        def first_block(at, step=step, bias_main=bias_main, bias_rest=bias_rest):
            main_a, main_b, rest = block(
                xm, xr, at, arrived[step, at], arrived[step, at + 1], wm, wr, wt, 0, bias_main[0], bias_rest[0]
            )
            row_a = 2 * group - 1 + 2 * at
            inside_a, inside_b = row_a >= 0, row_a + 1 < 2 * GROUPS
            low = lanes(rest.shape) < REST
            main_a = jnp.where(inside_a, main_a, 0.0)
            main_b = jnp.where(inside_b, main_b, 0.0)
            rest = jnp.where(low, jnp.where(inside_a, rest, 0.0), jnp.where(inside_b, rest, 0.0))
            hidden[at] = jnp.concatenate([main_a, main_b, rest], axis=1).astype(BF16)
            norm_pair(hidden[at], gain_main[1], gain_rest[1], hm, hr, at)

        own_copy(step).wait_recv()
        inner_copy(step).start()
        norm(1)
        inner_copy(step).wait_recv()
        near = 2 - 2 * core
        norm(near)
        first_block(1 - core)

        @pl.when(has_across)
        def _(step=step):
            across_copy(step).wait_recv()

        @pl.when(jnp.logical_not(has_across))
        def _(step=step):
            arrived[step, 2 * core] = jnp.zeros((PIX, PACK), BF16)

        norm(2 - near)
        first_block(core)
        main_a, main_b, rest = block(
            hm, hr, 0, hidden[0], hidden[1], wm, wr, wt, 1, bias_main[1], bias_rest[1]
        )
        h_a = hidden[0][:, MAIN : 2 * MAIN].astype(F32)
        h_b = hidden[1][:, :MAIN].astype(F32)
        low = lanes((PIX, 128)) < REST
        h_rest = roll_rest(jnp.where(low, hidden[1][:, 2 * MAIN :].astype(F32), hidden[0][:, 2 * MAIN :].astype(F32)))
        main_a = jnp.where(two_main, main_a, h_a)
        main_b = jnp.where(two_main, main_b, h_b)
        rest = jnp.where(two, rest, h_rest)
        if step + 1 < STEPS:
            packed[step + 1] = jnp.concatenate([main_a, main_b, rest], axis=1).astype(BF16)
            send(step + 1)
        else:
            for row, main in enumerate((main_a, main_b)):
                for f in range(FRAMES):
                    spot = slice(f * W, (f + 1) * W)
                    own = rest[spot, row * REST : (row + 1) * REST]
                    out[f, row] = jnp.concatenate([main[spot], own], axis=1).astype(BF16)

    for step in range(STEPS):
        own_copy(step).wait_send()
        inner_copy(step).wait_send()

        @pl.when(has_across)
        def _(step=step):
            across_copy(step).wait_send()


def body(state, bounds, timesteps, gains, spatial_weight, temporal_weight, time_weight):
    vmem = pl.BlockSpec(memory_space=pltpu.VMEM)
    smem = pl.BlockSpec(memory_space=pltpu.SMEM)
    hbm = pl.BlockSpec(memory_space=pl.ANY)
    out = pl.pallas_call(
        kernel,
        out_shape=jax.ShapeDtypeStruct((FRAMES, 2, W, C), BF16),
        in_specs=[vmem, smem, smem, vmem, hbm, hbm, hbm],
        out_specs=vmem,
        scratch_shapes=[
            pltpu.VMEM((2, 9, C, C), BF16),
            pltpu.VMEM((2, 3, C, C), BF16),
            pltpu.VMEM((2, C, C), F32),
            pltpu.VMEM((2, 3 * MAIN, NOUT), BF16),
            pltpu.VMEM((2, 2, MAIN, NOUT), BF16),
            pltpu.VMEM((2, PACK, PACK), BF16),
            pltpu.VMEM((STEPS, PIX, PACK), BF16),
            pltpu.VMEM((STEPS, 3, PIX, PACK), BF16),
            pltpu.VMEM((2, PIX, PACK), BF16),
            pltpu.VMEM((6, PIX, MAIN), BF16),
            pltpu.VMEM((3, PIX, 128), BF16),
            pltpu.VMEM((4, PIX, MAIN), BF16),
            pltpu.VMEM((2, PIX, 128), BF16),
            pltpu.SemaphoreType.DMA((2, 3)),
            pltpu.SemaphoreType.DMA((STEPS, 3)),
            pltpu.SemaphoreType.DMA((STEPS, 3)),
        ],
        compiler_params=pltpu.CompilerParams(
            collective_id=1, has_side_effects=True, vmem_limit_bytes=56 << 20
        ),
        cost_estimate=pl.CostEstimate(flops=4 << 30, bytes_accessed=6 << 20, transcendentals=1 << 20),
        name="cycle",
    )(
        state.reshape(FRAMES, 2, W, C),
        bounds,
        timesteps,
        gains.reshape(2, C),
        spatial_weight.reshape(2, 9, C, C),
        temporal_weight.reshape(2, 3, C, C),
        time_weight.reshape(2, C, C),
    )
    return out.reshape(1, FRAMES, 2, W * C)


def solution(mesh):
    placed = (
        P("segment", None, "rows", None),
        P(),
        P(),
        P("segment", None, None),
        P("segment", None, None, None, None, None),
        P("segment", None, None, None, None),
        P("segment", None, None, None),
    )
    return jax.shard_map(
        body,
        mesh=mesh,
        in_specs=placed,
        out_specs=P("segment", None, "rows", None),
        check_vma=False,
    )
```

```python
import math

import jax
import jax.numpy as jnp
from jax import lax
from jax.experimental import pallas as pl
from jax.experimental.pallas import tpu as pltpu
from jax.sharding import PartitionSpec as P

C = 320
W = 72
STEPS = 2
FRAMES = 2
SEGMENTS = 4
GROUPS = 64
MAIN = 256
REST = C - MAIN
PIX = FRAMES * W
PACK = 2 * MAIN + 2 * REST
NOUT = 4 * MAIN
PARTS = ((0, 48), (48, 48), (96, 48))
NEAR = ((0, 1, None, 2), (None, 0, 2, 1))
AFTER = ((2, None), (1, 2))
BEFORE = ((0, 1), (None, 0))
BEFORE_REVERSED = ((1, 0), (0, None))
MESH = pl.DeviceIdType.MESH
F32 = jnp.float32
BF16 = jnp.bfloat16


def lanes(shape):
    return lax.broadcasted_iota(jnp.int32, shape, len(shape) - 1)


def roll_rest(value):
    return pltpu.roll(value, REST, 1)


def norm_pair(pair, gain_main, gain_rest, xm, xr, first, second, at, spot=slice(None)):
    main_a = pair[:, :MAIN].astype(F32)
    main_b = pair[:, MAIN : 2 * MAIN].astype(F32)
    rest = pair[:, 2 * MAIN :].astype(F32)
    low = lanes(rest.shape) < REST
    square = rest * rest
    zero = jnp.zeros_like(square)

    def scale(main, own):
        both = main * main
        total = both[:, :128] + both[:, 128:] + own
        return lax.rsqrt(jnp.sum(total, axis=-1, keepdims=True) * (1.0 / C) + 1e-06)

    scale_a = scale(main_a, jnp.where(low, square, zero))
    scale_b = scale(main_b, jnp.where(low, zero, square))
    xm[first, spot] = (main_a * scale_a * gain_main).astype(BF16)
    xm[second, spot] = (main_b * scale_b * gain_main).astype(BF16)
    xr[at, spot] = (rest * jnp.where(low, scale_a, scale_b) * gain_rest).astype(BF16)


def dot(left, right):
    return jnp.dot(left, right, preferred_element_type=F32)


def columns(tile):
    return slice(tile * MAIN, (tile + 1) * MAIN)


def before_part(xm, row, rest, wm, wr, tile):
    cols = columns(tile)
    one = dot(jnp.concatenate([xm[row], xm[row + 1]], axis=1), wm[: 2 * MAIN, cols]) + dot(rest, wr[0, :, cols])
    two = dot(xm[row + 1], wm[:MAIN, cols]) + dot(rest, wr[1, :, cols])
    return jnp.concatenate([one, two], axis=0)


def after_part(xm, row, rest, wm, wr, tile):
    cols = columns(tile)
    one = dot(xm[row], wm[2 * MAIN :, cols]) + dot(rest, wr[0, :, cols])
    two = dot(jnp.concatenate([xm[row], xm[row + 1]], axis=1), wm[MAIN:, cols]) + dot(rest, wr[1, :, cols])
    return jnp.concatenate([one, two], axis=0)


def both_parts(xm, row, rest, wm, wr, tile):
    cols = columns(tile)
    left = jnp.concatenate([xm[row + dy : row + dy + 2].reshape(2 * PIX, MAIN) for dy in range(3)], axis=1)
    rests = jnp.concatenate([dot(rest, wr[0, :, cols]), dot(rest, wr[1, :, cols])], axis=0)
    return dot(left, wm[:, cols]) + rests


def finish(product, centre, wt, bias_main, bias_rest):
    spot = lax.rem(lax.broadcasted_iota(jnp.int32, (2 * PIX, 1), 0), W)
    first, last = spot == 0, spot == W - 1

    def from_before(value):
        return jnp.where(first, 0.0, pltpu.roll(value, 1, 0))

    def from_after(value):
        return jnp.where(last, 0.0, pltpu.roll(value, value.shape[0] - 1, 0))

    a_main = from_before(product(0)) + product(1) + from_after(product(2)) + bias_main
    z = product(3)
    sides = from_before(z[:, :128]) + from_after(z[:, 128:])
    middle = z[:, :128]
    low = lanes((PIX, 128)) < REST
    a_rest = jnp.where(
        low,
        sides[:PIX] + roll_rest(middle[:PIX]),
        roll_rest(sides[PIX:]) + middle[PIX:],
    ) + bias_rest

    def silu(value):
        return value * (0.5 * jnp.tanh(0.5 * value) + 0.5)

    u_main = silu(a_main)
    u_rest = silu(a_rest)
    low = lanes((W, 128)) < REST

    def transposed(first_half, second_half):
        return (
            jnp.where(low, first_half, roll_rest(second_half)),
            jnp.where(low, roll_rest(first_half), second_half),
        )

    rest_a, rest_b = transposed(u_rest[:W], u_rest[W:])
    mixed = jnp.concatenate(
        [
            jnp.concatenate([u_main[:W], u_main[PIX : PIX + W]], axis=0),
            jnp.concatenate([u_main[W:PIX], u_main[PIX + W :]], axis=0),
            jnp.concatenate([rest_a, rest_b], axis=0),
        ],
        axis=1,
    ).astype(BF16)
    v = dot(mixed, wt[...])
    v_a = jnp.concatenate([v[:W, :MAIN], v[:W, MAIN : 2 * MAIN]], axis=0)
    v_b = jnp.concatenate([v[W:, :MAIN], v[W:, MAIN : 2 * MAIN]], axis=0)
    v_rest = jnp.concatenate(transposed(v[:W, 2 * MAIN :], v[W:, 2 * MAIN :]), axis=0)
    h_a, h_b, h_rest = centre
    return h_a + a_main[:PIX] + v_a, h_b + a_main[PIX:] + v_b, h_rest + a_rest + v_rest


def kernel(
    state, bounds, timesteps, gains, spatial, temporal, time_weight,
    out,
    raw_s, raw_t, raw_b, wm, w_near, w_own, w_far, w_hid, wt, packed, arrived, hidden, xm, xr, hm, hr, zf, zh,
    load_sem, send_sem, recv_sem,
):
    segment = lax.axis_index("segment")
    group = lax.axis_index("rows")
    core = lax.rem(group, 2)
    behind, ahead = lax.rem(segment + SEGMENTS - 1, SEGMENTS), lax.rem(segment + 1, SEGMENTS)
    across = group - 1 + 2 * core
    inner = group + 1 - 2 * core
    has_across = (across >= 0) & (across < GROUPS)

    loads = []
    for slot in range(2):
        loads.append(
            (
                pltpu.make_async_copy(spatial.at[slot], raw_s.at[slot], load_sem.at[slot, 0]),
                pltpu.make_async_copy(temporal.at[slot], raw_t.at[slot], load_sem.at[slot, 1]),
                pltpu.make_async_copy(time_weight.at[slot], raw_b.at[slot], load_sem.at[slot, 2]),
            )
        )

    barrier = pltpu.get_barrier_semaphore()
    pl.semaphore_signal(barrier, inc=1, device_id=(behind, group), device_id_type=MESH)
    pl.semaphore_signal(barrier, inc=1, device_id=(segment, inner), device_id_type=MESH)

    @pl.when(has_across)
    def _():
        pl.semaphore_signal(barrier, inc=1, device_id=(segment, across), device_id_type=MESH)

    for load in loads[0] + loads[1]:
        load.start()

    rows = [[state[f, row].astype(F32) for f in range(FRAMES)] for row in (core, 1 - core)]
    main = [jnp.concatenate([x[:, :MAIN] for x in row], axis=0) for row in rows]
    rest = [jnp.concatenate([x[:, MAIN:] for x in row], axis=0) for row in rows]
    packed[0] = jnp.concatenate(main + rest, axis=1).astype(BF16)

    pl.semaphore_wait(barrier, 2 + has_across.astype(jnp.int32))

    def piece(step, kind, part, source, target, device):
        spot = pl.ds(*PARTS[part])
        return pltpu.make_async_remote_copy(
            source.at[spot], target.at[spot], send_sem.at[step, kind, part], recv_sem.at[step, kind, part],
            device_id=device, device_id_type=MESH,
        )

    def own_copy(step, part):
        return piece(step, 0, part, packed.at[step], arrived.at[step, 1], (ahead, group))

    def across_copy(step, part):
        return piece(step, 1, part, arrived.at[step, 1], arrived.at[step, 0], (segment, across))

    def inner_copy(step, part):
        return piece(step, 2, part, arrived.at[step, 1], arrived.at[step, 2], (segment, inner))

    parts = range(len(PARTS))
    for part in parts:
        own_copy(0, part).start()

    @pl.when(jnp.logical_not(has_across))
    def _():
        for step in range(STEPS):
            arrived[step, 0] = jnp.zeros((PIX, PACK), BF16)

    none = jnp.zeros((REST, NOUT), BF16)
    for slot in range(2):
        for load in loads[slot]:
            load.wait()
        for dy in range(3):
            taps = [3 * (dy + core * (2 - 2 * dy)) + dx for dx in range(3)]
            for dx in range(3):
                wm[slot, dy * MAIN : (dy + 1) * MAIN, columns(dx)] = raw_s[slot, taps[dx], :MAIN, :MAIN]
            rests = [raw_s[slot, tap, :, MAIN:] for tap in taps]
            rests = jnp.concatenate(rests + [jnp.zeros_like(rests[0])], axis=1)
            wm[slot, dy * MAIN : (dy + 1) * MAIN, columns(3)] = rests[:MAIN]
            tail = jnp.concatenate([raw_s[slot, tap, MAIN:, :MAIN] for tap in taps] + [rests[MAIN:]], axis=1)
            if slot == 0:
                places = ((w_near, NEAR), (w_own, AFTER), (w_far, BEFORE_REVERSED))
            else:
                places = ((w_own, AFTER), (w_hid, BEFORE))
            for ref, order in places:
                ref = ref.at[slot] if ref is w_own else ref
                for row in range(2):
                    for at, tap in enumerate(order[row]):
                        if tap == dy:
                            ref[row, at * REST : (at + 1) * REST] = tail
                        elif tap is None and dy == 0:
                            ref[row, at * REST : (at + 1) * REST] = none
        for f in range(FRAMES):
            for g in range(FRAMES):
                tap = f - g + 1
                wt[slot, f * MAIN : (f + 1) * MAIN, columns(g)] = raw_t[slot, tap, :MAIN, :MAIN]
                at = 2 * MAIN + f * REST
                wt[slot, at : at + REST, columns(g)] = raw_t[slot, tap, MAIN:, :MAIN]
            rests = jnp.concatenate([raw_t[slot, f - g + 1, :, MAIN:] for g in range(FRAMES)], axis=1)
            wt[slot, f * MAIN : (f + 1) * MAIN, 2 * MAIN :] = rests[:MAIN]
            at = 2 * MAIN + f * REST
            wt[slot, at : at + REST, 2 * MAIN :] = rests[MAIN:]

    half = C // 2
    number = lax.broadcasted_iota(jnp.int32, (8, half), 1).astype(F32)
    which = lax.broadcasted_iota(jnp.int32, (8, half), 0)
    t = jnp.where(which == 0, timesteps[0], timesteps[1]).astype(F32)
    angle = t * jnp.exp(-math.log(10000.0) * number / half)
    emb = jnp.concatenate([jnp.cos(angle), jnp.sin(angle)], axis=1)
    bias = [
        jnp.dot(emb, raw_b[slot], preferred_element_type=F32, precision=lax.Precision.HIGHEST) for slot in range(2)
    ]

    def twice(value):
        return jnp.concatenate([value, value], axis=1)

    gain_main = [gains[slot : slot + 1, :MAIN] for slot in range(2)]
    gain_rest = [twice(gains[slot : slot + 1, MAIN:]) for slot in range(2)]
    two = jnp.full((1, 128), bounds[segment + 1] - bounds[segment], jnp.int32) > 1
    two_main = jnp.concatenate([two, two], axis=1)
    low = lanes((PIX, 128)) < REST

    def first_of(pair):
        return pair[:, :MAIN].astype(F32)

    def second_of(pair):
        return pair[:, MAIN : 2 * MAIN].astype(F32)

    def rests_of(pair):
        return pair[:, 2 * MAIN :].astype(F32)

    for step in range(STEPS):
        bias_main = [bias[slot][step : step + 1, :MAIN] for slot in range(2)]
        bias_rest = [twice(bias[slot][step : step + 1, MAIN:]) for slot in range(2)]
        far, own, near = (arrived.at[step, at] for at in range(3))

        def keep(at, main_a, main_b, rest):
            hidden[at] = jnp.concatenate([main_a, main_b, rest], axis=1).astype(BF16)
            norm_pair(hidden[at], gain_main[1], gain_rest[1], hm, hr, 2 * at, 2 * at + 1, at)

        for part in parts:
            own_copy(step, part).wait_recv()
            inner_copy(step, part).start()

            @pl.when(has_across)
            def _(step=step, part=part):
                across_copy(step, part).start()

            begin, size = PARTS[part]
            spot = slice(begin, begin + size)
            norm_pair(own[spot], gain_main[0], gain_rest[0], xm, xr, 2, 3, 1, spot)
        for tile in range(4):
            zf[:, columns(tile)] = after_part(xm, 2, xr[1], wm.at[0], w_own.at[0], tile)

        for part in parts:
            inner_copy(step, part).wait_recv()
        norm_pair(near[...], gain_main[0], gain_rest[0], xm, xr, 5, 4, 2)
        rests = jnp.concatenate([xr[1], xr[2]], axis=1)
        centre = (second_of(own), second_of(near), jnp.where(low, roll_rest(rests_of(own)), rests_of(near)))
        results = finish(
            lambda tile: both_parts(xm, 2, rests, wm.at[0], w_near, tile), centre, wt.at[0], bias_main[0], bias_rest[0]
        )
        keep(1, *results)
        for tile in range(4):
            zh[:, columns(tile)] = after_part(hm, 2, hr[1], wm.at[1], w_own.at[1], tile)

        @pl.when(has_across)
        def _(step=step):
            for part in parts:
                across_copy(step, part).wait_recv()

        norm_pair(far[...], gain_main[0], gain_rest[0], xm, xr, 1, 0, 0)
        centre = (first_of(far), first_of(own), jnp.where(low, rests_of(far), roll_rest(rests_of(own))))
        main_a, main_b, rest = finish(
            lambda tile: zf[:, columns(tile)] + before_part(xm, 0, xr[0], wm.at[0], w_far, tile),
            centre, wt.at[0], bias_main[0], bias_rest[0],
        )
        keep(0, jnp.where(has_across, main_a, 0.0), main_b, jnp.where(low, jnp.where(has_across, rest, 0.0), rest))
        centre = (
            second_of(hidden.at[0]),
            first_of(hidden.at[1]),
            roll_rest(jnp.where(low, rests_of(hidden.at[1]), rests_of(hidden.at[0]))),
        )
        main_a, main_b, rest = finish(
            lambda tile: zh[:, columns(tile)] + before_part(hm, 0, hr[0], wm.at[1], w_hid, tile),
            centre, wt.at[1], bias_main[1], bias_rest[1],
        )
        main_a = jnp.where(two_main, main_a, centre[0])
        main_b = jnp.where(two_main, main_b, centre[1])
        rest = jnp.where(two, rest, centre[2])
        if step + 1 < STEPS:
            packed[step + 1] = jnp.concatenate([main_a, main_b, rest], axis=1).astype(BF16)
            for part in parts:
                own_copy(step + 1, part).start()
        else:
            for row, main in enumerate((main_a, main_b)):
                for f in range(FRAMES):
                    spot = slice(f * W, (f + 1) * W)
                    ends = rest[spot, row * REST : (row + 1) * REST]
                    out[f, core if row == 0 else 1 - core] = jnp.concatenate([main[spot], ends], axis=1).astype(BF16)

    for step in range(STEPS):
        for part in parts:
            own_copy(step, part).wait_send()
            inner_copy(step, part).wait_send()

        @pl.when(has_across)
        def _(step=step):
            for part in parts:
                across_copy(step, part).wait_send()


def body(state, bounds, timesteps, gains, spatial_weight, temporal_weight, time_weight):
    vmem = pl.BlockSpec(memory_space=pltpu.VMEM)
    smem = pl.BlockSpec(memory_space=pltpu.SMEM)
    hbm = pl.BlockSpec(memory_space=pl.ANY)
    out = pl.pallas_call(
        kernel,
        out_shape=jax.ShapeDtypeStruct((FRAMES, 2, W, C), BF16),
        in_specs=[vmem, smem, smem, vmem, hbm, hbm, hbm],
        out_specs=vmem,
        scratch_shapes=[
            pltpu.VMEM((2, 9, C, C), BF16),
            pltpu.VMEM((2, 3, C, C), BF16),
            pltpu.VMEM((2, C, C), F32),
            pltpu.VMEM((2, 3 * MAIN, NOUT), BF16),
            pltpu.VMEM((2, 4 * REST, NOUT), BF16),
            pltpu.VMEM((2, 2, 2 * REST, NOUT), BF16),
            pltpu.VMEM((2, 2 * REST, NOUT), BF16),
            pltpu.VMEM((2, 2 * REST, NOUT), BF16),
            pltpu.VMEM((2, PACK, PACK), BF16),
            pltpu.VMEM((STEPS, PIX, PACK), BF16),
            pltpu.VMEM((STEPS, 3, PIX, PACK), BF16),
            pltpu.VMEM((2, PIX, PACK), BF16),
            pltpu.VMEM((6, PIX, MAIN), BF16),
            pltpu.VMEM((3, PIX, 128), BF16),
            pltpu.VMEM((4, PIX, MAIN), BF16),
            pltpu.VMEM((2, PIX, 128), BF16),
            pltpu.VMEM((2 * PIX, NOUT), F32),
            pltpu.VMEM((2 * PIX, NOUT), F32),
            pltpu.SemaphoreType.DMA((2, 3)),
            pltpu.SemaphoreType.DMA((STEPS, 3, len(PARTS))),
            pltpu.SemaphoreType.DMA((STEPS, 3, len(PARTS))),
        ],
        compiler_params=pltpu.CompilerParams(
            collective_id=1, has_side_effects=True, vmem_limit_bytes=56 << 20
        ),
        cost_estimate=pl.CostEstimate(flops=4 << 30, bytes_accessed=6 << 20, transcendentals=1 << 20),
        name="cycle",
    )(
        state.reshape(FRAMES, 2, W, C),
        bounds,
        timesteps,
        gains.reshape(2, C),
        spatial_weight.reshape(2, 9, C, C),
        temporal_weight.reshape(2, 3, C, C),
        time_weight.reshape(2, C, C),
    )
    return out.reshape(1, FRAMES, 2, W * C)


def solution(mesh):
    placed = (
        P("segment", None, "rows", None),
        P(),
        P(),
        P("segment", None, None),
        P("segment", None, None, None, None, None),
        P("segment", None, None, None, None),
        P("segment", None, None, None),
    )
    return jax.shard_map(
        body,
        mesh=mesh,
        in_specs=placed,
        out_specs=P("segment", None, "rows", None),
        check_vma=False,
    )
```

```python
import math

import jax
import jax.numpy as jnp
from jax import lax
from jax.experimental import pallas as pl
from jax.experimental.pallas import tpu as pltpu
from jax.sharding import PartitionSpec as P

C = 320
W = 72
STEPS = 2
FRAMES = 2
SEGMENTS = 4
GROUPS = 64
MAIN = 256
REST = C - MAIN
PIX = FRAMES * W
PACK = 2 * MAIN + 2 * REST
TILES = 2 * C // 128
NOUT = 4 * MAIN
PARTS = ((0, 48), (48, 48), (96, 48))
NEAR = ((0, 1, None, 2), (None, 0, 2, 1))
AFTER = ((2, None), (1, 2))
BEFORE = ((0, 1), (None, 0))
BEFORE_REVERSED = ((1, 0), (0, None))
MESH = pl.DeviceIdType.MESH
F32 = jnp.float32
BF16 = jnp.bfloat16


def lanes(shape):
    return lax.broadcasted_iota(jnp.int32, shape, len(shape) - 1)


def roll_rest(value):
    return pltpu.roll(value, REST, 1)


def norm_pair(pair, gain_main, gain_rest, xm, xr, first, second, at, spot=slice(None)):
    main_a = pair[:, :MAIN].astype(F32)
    main_b = pair[:, MAIN : 2 * MAIN].astype(F32)
    rest = pair[:, 2 * MAIN :].astype(F32)
    low = lanes(rest.shape) < REST
    square = rest * rest
    zero = jnp.zeros_like(square)

    def scale(main, own):
        both = main * main
        total = both[:, :128] + both[:, 128:] + own
        return lax.rsqrt(jnp.sum(total, axis=-1, keepdims=True) * (1.0 / C) + 1e-06)

    scale_a = scale(main_a, jnp.where(low, square, zero))
    scale_b = scale(main_b, jnp.where(low, zero, square))
    xm[first, spot] = (main_a * scale_a * gain_main).astype(BF16)
    xm[second, spot] = (main_b * scale_b * gain_main).astype(BF16)
    xr[at, spot] = (rest * jnp.where(low, scale_a, scale_b) * gain_rest).astype(BF16)


def dot(left, right):
    return jnp.dot(left, right, preferred_element_type=F32)


def columns(tile):
    return slice(tile * MAIN, (tile + 1) * MAIN)


def before_part(xm, row, rest, wm, wr, tile):
    cols = columns(tile)
    one = dot(jnp.concatenate([xm[row], xm[row + 1]], axis=1), wm[: 2 * MAIN, cols]) + dot(rest, wr[0, :, cols])
    two = dot(xm[row + 1], wm[:MAIN, cols]) + dot(rest, wr[1, :, cols])
    return jnp.concatenate([one, two], axis=0)


def after_part(xm, row, rest, wm, wr, tile):
    cols = columns(tile)
    one = dot(xm[row], wm[2 * MAIN :, cols]) + dot(rest, wr[0, :, cols])
    two = dot(jnp.concatenate([xm[row], xm[row + 1]], axis=1), wm[MAIN:, cols]) + dot(rest, wr[1, :, cols])
    return jnp.concatenate([one, two], axis=0)


def both_parts(xm, row, rest, wm, wr, tile):
    cols = columns(tile)
    left = jnp.concatenate([xm[row + dy : row + dy + 2].reshape(2 * PIX, MAIN) for dy in range(3)], axis=1)
    rests = jnp.concatenate([dot(rest, wr[0, :, cols]), dot(rest, wr[1, :, cols])], axis=0)
    return dot(left, wm[:, cols]) + rests


def finish(product, centre, wt, bias_main, bias_rest):
    spot = lax.rem(lax.broadcasted_iota(jnp.int32, (2 * PIX, 1), 0), W)
    first, last = spot == 0, spot == W - 1

    def from_before(value):
        return jnp.where(first, 0.0, pltpu.roll(value, 1, 0))

    def from_after(value):
        return jnp.where(last, 0.0, pltpu.roll(value, value.shape[0] - 1, 0))

    a_main = from_before(product(0)) + product(1) + from_after(product(2)) + bias_main
    z = product(3)
    sides = from_before(z[:, :128]) + from_after(z[:, 128:])
    middle = z[:, :128]
    low = lanes((PIX, 128)) < REST
    a_rest = jnp.where(
        low,
        sides[:PIX] + roll_rest(middle[:PIX]),
        roll_rest(sides[PIX:]) + middle[PIX:],
    ) + bias_rest

    def silu(value):
        return value * (0.5 * jnp.tanh(0.5 * value) + 0.5)

    u_main = silu(a_main)
    u_rest = silu(a_rest)
    low = lanes((W, 128)) < REST

    def transposed(first_half, second_half):
        return (
            jnp.where(low, first_half, roll_rest(second_half)),
            jnp.where(low, roll_rest(first_half), second_half),
        )

    rest_a, rest_b = transposed(u_rest[:W], u_rest[W:])
    mixed = jnp.concatenate(
        [
            jnp.concatenate([u_main[:W], u_main[PIX : PIX + W]], axis=0),
            jnp.concatenate([u_main[W:PIX], u_main[PIX + W :]], axis=0),
            jnp.concatenate([rest_a, rest_b], axis=0),
        ],
        axis=1,
    ).astype(BF16)
    v = dot(mixed, wt[...])
    v_a = jnp.concatenate([v[:W, :MAIN], v[:W, MAIN : 2 * MAIN]], axis=0)
    v_b = jnp.concatenate([v[W:, :MAIN], v[W:, MAIN : 2 * MAIN]], axis=0)
    v_rest = jnp.concatenate(transposed(v[:W, 2 * MAIN :], v[W:, 2 * MAIN :]), axis=0)
    h_a, h_b, h_rest = centre
    return h_a + a_main[:PIX] + v_a, h_b + a_main[PIX:] + v_b, h_rest + a_rest + v_rest


def kernel(
    state, bounds, timesteps, gains, spatial, temporal, time_weight,
    out,
    raw_x, strip, pixels, raw_s, raw_t, raw_b, wm, w_near, w_own, w_far, w_hid, wt, packed, arrived, hidden, xm, xr, hm, hr, zf, zh,
    load_sem, send_sem, recv_sem,
):
    segment = lax.axis_index("segment")
    group = lax.axis_index("rows")
    core = lax.rem(group, 2)
    behind, ahead = lax.rem(segment + SEGMENTS - 1, SEGMENTS), lax.rem(segment + 1, SEGMENTS)
    across = group - 1 + 2 * core
    inner = group + 1 - 2 * core
    has_across = (across >= 0) & (across < GROUPS)

    loads = []
    for slot in range(2):
        loads.append(
            (
                pltpu.make_async_copy(spatial.at[slot], raw_s.at[slot], load_sem.at[slot, 0]),
                pltpu.make_async_copy(temporal.at[slot], raw_t.at[slot], load_sem.at[slot, 1]),
                pltpu.make_async_copy(time_weight.at[slot], raw_b.at[slot], load_sem.at[slot, 2]),
            )
        )

    barrier = pltpu.get_barrier_semaphore()
    pl.semaphore_signal(barrier, inc=1, device_id=(behind, group), device_id_type=MESH)
    pl.semaphore_signal(barrier, inc=1, device_id=(segment, inner), device_id_type=MESH)

    @pl.when(has_across)
    def _():
        pl.semaphore_signal(barrier, inc=1, device_id=(segment, across), device_id_type=MESH)

    state_load = pltpu.make_async_copy(state.at[0], raw_x, load_sem.at[2, 0])
    for load in (state_load, *loads[0], *loads[1]):
        load.start()

    state_load.wait()
    low_half = lanes((W // 2, 128)) < REST
    for f in range(FRAMES):
        for pair in range(W // 2):
            for k in range(TILES):
                begin = 2 * C * pair + 128 * k
                strip[f, k, 2 * pair : 2 * pair + 2] = raw_x[f, :, begin : begin + 128].astype(F32)
        for row, at in ((0, core), (1, 1 - core)):
            own = [strip[f, k, pl.ds(row, W // 2, stride=2)] for k in range(TILES)]
            swapped = [None, None] + [roll_rest(tile) for tile in own[2:]]
            odd = [jnp.where(low_half, swapped[2 + k], swapped[min(3 + k, 4)]) for k in range(3)]
            for k in range(3):
                pixels[at, k, pl.ds(f * W, W // 2, stride=2)] = own[k]
                pixels[at, k, pl.ds(f * W + 1, W // 2, stride=2)] = odd[k]
    rest = jnp.where(lanes((PIX, 128)) < REST, pixels[0, 2], roll_rest(pixels[1, 2]))
    packed[0] = jnp.concatenate([pixels[at, k] for at in range(2) for k in range(2)] + [rest], axis=1).astype(BF16)

    pl.semaphore_wait(barrier, 2 + has_across.astype(jnp.int32))

    def piece(step, kind, part, source, target, device):
        spot = pl.ds(*PARTS[part])
        return pltpu.make_async_remote_copy(
            source.at[spot], target.at[spot], send_sem.at[step, kind, part], recv_sem.at[step, kind, part],
            device_id=device, device_id_type=MESH,
        )

    def own_copy(step, part):
        return piece(step, 0, part, packed.at[step], arrived.at[step, 1], (ahead, group))

    def across_copy(step, part):
        return piece(step, 1, part, arrived.at[step, 1], arrived.at[step, 0], (segment, across))

    def inner_copy(step, part):
        return piece(step, 2, part, arrived.at[step, 1], arrived.at[step, 2], (segment, inner))

    parts = range(len(PARTS))
    for part in parts:
        own_copy(0, part).start()

    @pl.when(jnp.logical_not(has_across))
    def _():
        for step in range(STEPS):
            arrived[step, 0] = jnp.zeros((PIX, PACK), BF16)

    none = jnp.zeros((REST, NOUT), BF16)
    for slot in range(2):
        for load in loads[slot]:
            load.wait()
        for dy in range(3):
            taps = [3 * (dy + core * (2 - 2 * dy)) + dx for dx in range(3)]
            for dx in range(3):
                wm[slot, dy * MAIN : (dy + 1) * MAIN, columns(dx)] = raw_s[slot, taps[dx], :MAIN, :MAIN]
            rests = [raw_s[slot, tap, :, MAIN:] for tap in taps]
            rests = jnp.concatenate(rests + [jnp.zeros_like(rests[0])], axis=1)
            wm[slot, dy * MAIN : (dy + 1) * MAIN, columns(3)] = rests[:MAIN]
            tail = jnp.concatenate([raw_s[slot, tap, MAIN:, :MAIN] for tap in taps] + [rests[MAIN:]], axis=1)
            if slot == 0:
                places = ((w_near, NEAR), (w_own, AFTER), (w_far, BEFORE_REVERSED))
            else:
                places = ((w_own, AFTER), (w_hid, BEFORE))
            for ref, order in places:
                ref = ref.at[slot] if ref is w_own else ref
                for row in range(2):
                    for at, tap in enumerate(order[row]):
                        if tap == dy:
                            ref[row, at * REST : (at + 1) * REST] = tail
                        elif tap is None and dy == 0:
                            ref[row, at * REST : (at + 1) * REST] = none
        for f in range(FRAMES):
            for g in range(FRAMES):
                tap = f - g + 1
                wt[slot, f * MAIN : (f + 1) * MAIN, columns(g)] = raw_t[slot, tap, :MAIN, :MAIN]
                at = 2 * MAIN + f * REST
                wt[slot, at : at + REST, columns(g)] = raw_t[slot, tap, MAIN:, :MAIN]
            rests = jnp.concatenate([raw_t[slot, f - g + 1, :, MAIN:] for g in range(FRAMES)], axis=1)
            wt[slot, f * MAIN : (f + 1) * MAIN, 2 * MAIN :] = rests[:MAIN]
            at = 2 * MAIN + f * REST
            wt[slot, at : at + REST, 2 * MAIN :] = rests[MAIN:]

    half = C // 2
    number = lax.broadcasted_iota(jnp.int32, (8, half), 1).astype(F32)
    which = lax.broadcasted_iota(jnp.int32, (8, half), 0)
    t = jnp.where(which == 0, timesteps[0], timesteps[1]).astype(F32)
    angle = t * jnp.exp(-math.log(10000.0) * number / half)
    emb = jnp.concatenate([jnp.cos(angle), jnp.sin(angle)], axis=1)
    bias = [
        jnp.dot(emb, raw_b[slot], preferred_element_type=F32, precision=lax.Precision.HIGHEST) for slot in range(2)
    ]

    def twice(value):
        return jnp.concatenate([value, value], axis=1)

    gain_main = [gains[slot : slot + 1, :MAIN] for slot in range(2)]
    gain_rest = [twice(gains[slot : slot + 1, MAIN:]) for slot in range(2)]
    two = jnp.full((1, 128), bounds[segment + 1] - bounds[segment], jnp.int32) > 1
    two_main = jnp.concatenate([two, two], axis=1)
    low = lanes((PIX, 128)) < REST

    def first_of(pair):
        return pair[:, :MAIN].astype(F32)

    def second_of(pair):
        return pair[:, MAIN : 2 * MAIN].astype(F32)

    def rests_of(pair):
        return pair[:, 2 * MAIN :].astype(F32)

    for step in range(STEPS):
        bias_main = [bias[slot][step : step + 1, :MAIN] for slot in range(2)]
        bias_rest = [twice(bias[slot][step : step + 1, MAIN:]) for slot in range(2)]
        far, own, near = (arrived.at[step, at] for at in range(3))

        def keep(at, main_a, main_b, rest):
            hidden[at] = jnp.concatenate([main_a, main_b, rest], axis=1).astype(BF16)
            norm_pair(hidden[at], gain_main[1], gain_rest[1], hm, hr, 2 * at, 2 * at + 1, at)

        for part in parts:
            own_copy(step, part).wait_recv()
            inner_copy(step, part).start()

            @pl.when(has_across)
            def _(step=step, part=part):
                across_copy(step, part).start()

            begin, size = PARTS[part]
            spot = slice(begin, begin + size)
            norm_pair(own[spot], gain_main[0], gain_rest[0], xm, xr, 2, 3, 1, spot)
        for tile in range(4):
            zf[:, columns(tile)] = after_part(xm, 2, xr[1], wm.at[0], w_own.at[0], tile)

        for part in parts:
            inner_copy(step, part).wait_recv()
        norm_pair(near[...], gain_main[0], gain_rest[0], xm, xr, 5, 4, 2)
        rests = jnp.concatenate([xr[1], xr[2]], axis=1)
        centre = (second_of(own), second_of(near), jnp.where(low, roll_rest(rests_of(own)), rests_of(near)))
        results = finish(
            lambda tile: both_parts(xm, 2, rests, wm.at[0], w_near, tile), centre, wt.at[0], bias_main[0], bias_rest[0]
        )
        keep(1, *results)
        for tile in range(4):
            zh[:, columns(tile)] = after_part(hm, 2, hr[1], wm.at[1], w_own.at[1], tile)

        @pl.when(has_across)
        def _(step=step):
            for part in parts:
                across_copy(step, part).wait_recv()

        norm_pair(far[...], gain_main[0], gain_rest[0], xm, xr, 1, 0, 0)
        centre = (first_of(far), first_of(own), jnp.where(low, rests_of(far), roll_rest(rests_of(own))))
        main_a, main_b, rest = finish(
            lambda tile: zf[:, columns(tile)] + before_part(xm, 0, xr[0], wm.at[0], w_far, tile),
            centre, wt.at[0], bias_main[0], bias_rest[0],
        )
        keep(0, jnp.where(has_across, main_a, 0.0), main_b, jnp.where(low, jnp.where(has_across, rest, 0.0), rest))
        centre = (
            second_of(hidden.at[0]),
            first_of(hidden.at[1]),
            roll_rest(jnp.where(low, rests_of(hidden.at[1]), rests_of(hidden.at[0]))),
        )
        main_a, main_b, rest = finish(
            lambda tile: zh[:, columns(tile)] + before_part(hm, 0, hr[0], wm.at[1], w_hid, tile),
            centre, wt.at[1], bias_main[1], bias_rest[1],
        )
        main_a = jnp.where(two_main, main_a, centre[0])
        main_b = jnp.where(two_main, main_b, centre[1])
        rest = jnp.where(two, rest, centre[2])
        if step + 1 < STEPS:
            packed[step + 1] = jnp.concatenate([main_a, main_b, rest], axis=1).astype(BF16)
            for part in parts:
                own_copy(step + 1, part).start()
        else:
            for at, (main, ends) in enumerate(((main_a, rest), (main_b, roll_rest(rest)))):
                pixels[at, 0], pixels[at, 1], pixels[at, 2] = main[:, :128], main[:, 128:], ends
            for f in range(FRAMES):
                for row, at in ((0, core), (1, 1 - core)):
                    even, odd = (
                        [pixels[at, k, pl.ds(f * W + one, W // 2, stride=2)] for k in range(3)] for one in range(2)
                    )
                    odd = [roll_rest(tile) for tile in odd]
                    own = [even[0], even[1]]
                    own += [jnp.where(low_half, one, two) for one, two in ((even[2], odd[0]), odd[:2], odd[1:])]
                    for k in range(TILES):
                        strip[f, k, pl.ds(row, W // 2, stride=2)] = own[k]
                for pair in range(W // 2):
                    for k in range(TILES):
                        begin = 2 * C * pair + 128 * k
                        out[0, f, :, begin : begin + 128] = strip[f, k, 2 * pair : 2 * pair + 2].astype(BF16)

    for step in range(STEPS):
        for part in parts:
            own_copy(step, part).wait_send()
            inner_copy(step, part).wait_send()

        @pl.when(has_across)
        def _(step=step):
            for part in parts:
                across_copy(step, part).wait_send()


def body(state, bounds, timesteps, gains, spatial_weight, temporal_weight, time_weight):
    vmem = pl.BlockSpec(memory_space=pltpu.VMEM)
    smem = pl.BlockSpec(memory_space=pltpu.SMEM)
    hbm = pl.BlockSpec(memory_space=pl.ANY)
    return pl.pallas_call(
        kernel,
        out_shape=jax.ShapeDtypeStruct((1, FRAMES, 2, W * C), BF16),
        in_specs=[hbm, smem, smem, vmem, hbm, hbm, hbm],
        out_specs=vmem,
        scratch_shapes=[
            pltpu.VMEM((FRAMES, 2, W * C), BF16),
            pltpu.VMEM((FRAMES, TILES, W, 128), F32),
            pltpu.VMEM((2, 3, PIX, 128), F32),
            pltpu.VMEM((2, 9, C, C), BF16),
            pltpu.VMEM((2, 3, C, C), BF16),
            pltpu.VMEM((2, C, C), F32),
            pltpu.VMEM((2, 3 * MAIN, NOUT), BF16),
            pltpu.VMEM((2, 4 * REST, NOUT), BF16),
            pltpu.VMEM((2, 2, 2 * REST, NOUT), BF16),
            pltpu.VMEM((2, 2 * REST, NOUT), BF16),
            pltpu.VMEM((2, 2 * REST, NOUT), BF16),
            pltpu.VMEM((2, PACK, PACK), BF16),
            pltpu.VMEM((STEPS, PIX, PACK), BF16),
            pltpu.VMEM((STEPS, 3, PIX, PACK), BF16),
            pltpu.VMEM((2, PIX, PACK), BF16),
            pltpu.VMEM((6, PIX, MAIN), BF16),
            pltpu.VMEM((3, PIX, 128), BF16),
            pltpu.VMEM((4, PIX, MAIN), BF16),
            pltpu.VMEM((2, PIX, 128), BF16),
            pltpu.VMEM((2 * PIX, NOUT), F32),
            pltpu.VMEM((2 * PIX, NOUT), F32),
            pltpu.SemaphoreType.DMA((3, 3)),
            pltpu.SemaphoreType.DMA((STEPS, 3, len(PARTS))),
            pltpu.SemaphoreType.DMA((STEPS, 3, len(PARTS))),
        ],
        compiler_params=pltpu.CompilerParams(
            collective_id=1, has_side_effects=True, vmem_limit_bytes=56 << 20
        ),
        cost_estimate=pl.CostEstimate(flops=4 << 30, bytes_accessed=6 << 20, transcendentals=1 << 20),
        name="cycle",
    )(
        state,
        bounds,
        timesteps,
        gains.reshape(2, C),
        spatial_weight.reshape(2, 9, C, C),
        temporal_weight.reshape(2, 3, C, C),
        time_weight.reshape(2, C, C),
    )


def solution(mesh):
    placed = (
        P("segment", None, "rows", None),
        P(),
        P(),
        P("segment", None, None),
        P("segment", None, None, None, None, None),
        P("segment", None, None, None, None),
        P("segment", None, None, None),
    )
    return jax.shard_map(
        body,
        mesh=mesh,
        in_specs=placed,
        out_specs=P("segment", None, "rows", None),
        check_vma=False,
    )
```

```python
import math

import jax
import jax.numpy as jnp
from jax import lax
from jax.experimental import pallas as pl
from jax.experimental.pallas import tpu as pltpu
from jax.sharding import PartitionSpec as P

C = 320
W = 72
STEPS = 2
FRAMES = 2
SEGMENTS = 4
GROUPS = 64
MAIN = 256
REST = C - MAIN
PIX = FRAMES * W
PACK = 2 * MAIN + 2 * REST
TILES = 2 * C // 128
NOUT = 4 * MAIN
PARTS = ((0, 48), (48, 48), (96, 48))
NEAR = ((0, 1, None, 2), (None, 0, 2, 1))
AFTER = ((2, None), (1, 2))
BEFORE = ((0, 1), (None, 0))
BEFORE_REVERSED = ((1, 0), (0, None))
MESH = pl.DeviceIdType.MESH
F32 = jnp.float32
BF16 = jnp.bfloat16


def lanes(shape):
    return lax.broadcasted_iota(jnp.int32, shape, len(shape) - 1)


def roll_rest(value):
    return pltpu.roll(value, REST, 1)


def norm_pair(pair, gain_main, gain_rest, xm, xr, first, second, at, spot=slice(None)):
    main_a = pair[:, :MAIN].astype(F32)
    main_b = pair[:, MAIN : 2 * MAIN].astype(F32)
    rest = pair[:, 2 * MAIN :].astype(F32)
    low = lanes(rest.shape) < REST
    square = rest * rest
    zero = jnp.zeros_like(square)

    def scale(main, own):
        both = main * main
        total = both[:, :128] + both[:, 128:] + own
        return lax.rsqrt(jnp.sum(total, axis=-1, keepdims=True) * (1.0 / C) + 1e-06)

    scale_a = scale(main_a, jnp.where(low, square, zero))
    scale_b = scale(main_b, jnp.where(low, zero, square))
    xm[first, spot] = (main_a * scale_a * gain_main).astype(BF16)
    xm[second, spot] = (main_b * scale_b * gain_main).astype(BF16)
    xr[at, spot] = (rest * jnp.where(low, scale_a, scale_b) * gain_rest).astype(BF16)


def first_of(pair):
    return pair[:, :MAIN].astype(F32)


def second_of(pair):
    return pair[:, MAIN : 2 * MAIN].astype(F32)


def rests_of(pair):
    return pair[:, 2 * MAIN :].astype(F32)


def dot(left, right):
    return jnp.dot(left, right, preferred_element_type=F32)


def columns(tile):
    return slice(tile * MAIN, (tile + 1) * MAIN)


def before_part(xm, row, rest, wm, wr, tile):
    cols = columns(tile)
    one = dot(jnp.concatenate([xm[row], xm[row + 1]], axis=1), wm[: 2 * MAIN, cols]) + dot(rest, wr[0, :, cols])
    two = dot(xm[row + 1], wm[:MAIN, cols]) + dot(rest, wr[1, :, cols])
    return jnp.concatenate([one, two], axis=0)


def after_part(xm, row, rest, wm, wr, tile):
    cols = columns(tile)
    one = dot(xm[row], wm[2 * MAIN :, cols]) + dot(rest, wr[0, :, cols])
    two = dot(jnp.concatenate([xm[row], xm[row + 1]], axis=1), wm[MAIN:, cols]) + dot(rest, wr[1, :, cols])
    return jnp.concatenate([one, two], axis=0)


def both_parts(xm, row, rest, wm, wr, tile):
    cols = columns(tile)
    left = jnp.concatenate([xm[row + dy : row + dy + 2].reshape(2 * PIX, MAIN) for dy in range(3)], axis=1)
    rests = jnp.concatenate([dot(rest, wr[0, :, cols]), dot(rest, wr[1, :, cols])], axis=0)
    return dot(left, wm[:, cols]) + rests


def finish(product, centre, wt, bias_main, bias_rest):
    spot = lax.rem(lax.broadcasted_iota(jnp.int32, (2 * PIX, 1), 0), W)
    first, last = spot == 0, spot == W - 1

    def from_before(value):
        return jnp.where(first, 0.0, pltpu.roll(value, 1, 0))

    def from_after(value):
        return jnp.where(last, 0.0, pltpu.roll(value, value.shape[0] - 1, 0))

    a_main = from_before(product(0)) + product(1) + from_after(product(2)) + bias_main
    z = product(3)
    sides = from_before(z[:, :128]) + from_after(z[:, 128:])
    middle = z[:, :128]
    low = lanes((PIX, 128)) < REST
    a_rest = jnp.where(
        low,
        sides[:PIX] + roll_rest(middle[:PIX]),
        roll_rest(sides[PIX:]) + middle[PIX:],
    ) + bias_rest

    def silu(value):
        return value * (0.5 * jnp.tanh(0.5 * value) + 0.5)

    u_main = silu(a_main)
    u_rest = silu(a_rest)
    low = lanes((W, 128)) < REST

    def transposed(first_half, second_half):
        return (
            jnp.where(low, first_half, roll_rest(second_half)),
            jnp.where(low, roll_rest(first_half), second_half),
        )

    rest_a, rest_b = transposed(u_rest[:W], u_rest[W:])
    mixed = jnp.concatenate(
        [
            jnp.concatenate([u_main[:W], u_main[PIX : PIX + W]], axis=0),
            jnp.concatenate([u_main[W:PIX], u_main[PIX + W :]], axis=0),
            jnp.concatenate([rest_a, rest_b], axis=0),
        ],
        axis=1,
    ).astype(BF16)
    v = dot(mixed, wt[...])
    v_a = jnp.concatenate([v[:W, :MAIN], v[:W, MAIN : 2 * MAIN]], axis=0)
    v_b = jnp.concatenate([v[W:, :MAIN], v[W:, MAIN : 2 * MAIN]], axis=0)
    v_rest = jnp.concatenate(transposed(v[:W, 2 * MAIN :], v[W:, 2 * MAIN :]), axis=0)
    h_a, h_b, h_rest = centre
    return h_a + a_main[:PIX] + v_a, h_b + a_main[PIX:] + v_b, h_rest + a_rest + v_rest


def kernel(
    state, bounds, timesteps, gains, spatial, temporal, time_weight,
    out,
    raw_x, strip, pixels, raw_s, raw_t, raw_b, wm, w_near, w_own, w_far, w_hid, wt, packed, arrived, hidden, xm, xr, hm, hr, zf, zh,
    load_sem, send_sem, recv_sem,
):
    segment = lax.axis_index("segment")
    group = lax.axis_index("rows")
    core = lax.rem(group, 2)
    behind, ahead = lax.rem(segment + SEGMENTS - 1, SEGMENTS), lax.rem(segment + 1, SEGMENTS)
    across = group - 1 + 2 * core
    inner = group + 1 - 2 * core
    has_across = (across >= 0) & (across < GROUPS)

    loads = []
    for slot in range(2):
        loads.append(
            (
                pltpu.make_async_copy(spatial.at[slot], raw_s.at[slot], load_sem.at[slot, 0]),
                pltpu.make_async_copy(temporal.at[slot], raw_t.at[slot], load_sem.at[slot, 1]),
                pltpu.make_async_copy(time_weight.at[slot], raw_b.at[slot], load_sem.at[slot, 2]),
            )
        )

    barrier = pltpu.get_barrier_semaphore()
    pl.semaphore_signal(barrier, inc=1, device_id=(behind, group), device_id_type=MESH)
    pl.semaphore_signal(barrier, inc=1, device_id=(segment, inner), device_id_type=MESH)

    @pl.when(has_across)
    def _():
        pl.semaphore_signal(barrier, inc=1, device_id=(segment, across), device_id_type=MESH)

    state_load = pltpu.make_async_copy(state.at[0], raw_x, load_sem.at[2, 0])
    for load in (state_load, *loads[0], *loads[1]):
        load.start()

    state_load.wait()
    low_half = lanes((W // 2, 128)) < REST
    for f in range(FRAMES):
        for pair in range(W // 2):
            for k in range(TILES):
                begin = 2 * C * pair + 128 * k
                strip[f, k, 2 * pair : 2 * pair + 2] = raw_x[f, :, begin : begin + 128].astype(F32)
        for row, at in ((0, core), (1, 1 - core)):
            own = [strip[f, k, pl.ds(row, W // 2, stride=2)] for k in range(TILES)]
            swapped = [None, None] + [roll_rest(tile) for tile in own[2:]]
            odd = [jnp.where(low_half, swapped[2 + k], swapped[min(3 + k, 4)]) for k in range(3)]
            for k in range(3):
                pixels[at, k, pl.ds(f * W, W // 2, stride=2)] = own[k]
                pixels[at, k, pl.ds(f * W + 1, W // 2, stride=2)] = odd[k]
    rest = jnp.where(lanes((PIX, 128)) < REST, pixels[0, 2], roll_rest(pixels[1, 2]))
    packed[0] = jnp.concatenate([pixels[at, k] for at in range(2) for k in range(2)] + [rest], axis=1).astype(BF16)

    pl.semaphore_wait(barrier, 2 + has_across.astype(jnp.int32))

    def piece(step, kind, part, source, target, device):
        spot = pl.ds(*PARTS[part])
        return pltpu.make_async_remote_copy(
            source.at[spot], target.at[spot], send_sem.at[step, kind, part], recv_sem.at[step, kind, part],
            device_id=device, device_id_type=MESH,
        )

    def own_copy(step, part):
        return piece(step, 0, part, packed.at[step], arrived.at[step, 1], (ahead, group))

    def across_copy(step, part):
        return piece(step, 1, part, arrived.at[step, 1], arrived.at[step, 0], (segment, across))

    def inner_copy(step, part):
        return piece(step, 2, part, arrived.at[step, 1], arrived.at[step, 2], (segment, inner))

    parts = range(len(PARTS))
    for part in parts:
        own_copy(0, part).start()

    @pl.when(jnp.logical_not(has_across))
    def _():
        for step in range(STEPS):
            arrived[step, 0] = jnp.zeros((PIX, PACK), BF16)

    none = jnp.zeros((REST, NOUT), BF16)
    for slot in range(2):
        for load in loads[slot]:
            load.wait()
        for dy in range(3):
            taps = [3 * (dy + core * (2 - 2 * dy)) + dx for dx in range(3)]
            for dx in range(3):
                wm[slot, dy * MAIN : (dy + 1) * MAIN, columns(dx)] = raw_s[slot, taps[dx], :MAIN, :MAIN]
            rests = [raw_s[slot, tap, :, MAIN:] for tap in taps]
            rests = jnp.concatenate(rests + [jnp.zeros_like(rests[0])], axis=1)
            wm[slot, dy * MAIN : (dy + 1) * MAIN, columns(3)] = rests[:MAIN]
            tail = jnp.concatenate([raw_s[slot, tap, MAIN:, :MAIN] for tap in taps] + [rests[MAIN:]], axis=1)
            if slot == 0:
                places = ((w_near, NEAR), (w_own, AFTER), (w_far, BEFORE_REVERSED))
            else:
                places = ((w_own, AFTER), (w_hid, BEFORE))
            for ref, order in places:
                ref = ref.at[slot] if ref is w_own else ref
                for row in range(2):
                    for at, tap in enumerate(order[row]):
                        if tap == dy:
                            ref[row, at * REST : (at + 1) * REST] = tail
                        elif tap is None and dy == 0:
                            ref[row, at * REST : (at + 1) * REST] = none
        for f in range(FRAMES):
            for g in range(FRAMES):
                tap = f - g + 1
                wt[slot, f * MAIN : (f + 1) * MAIN, columns(g)] = raw_t[slot, tap, :MAIN, :MAIN]
                at = 2 * MAIN + f * REST
                wt[slot, at : at + REST, columns(g)] = raw_t[slot, tap, MAIN:, :MAIN]
            rests = jnp.concatenate([raw_t[slot, f - g + 1, :, MAIN:] for g in range(FRAMES)], axis=1)
            wt[slot, f * MAIN : (f + 1) * MAIN, 2 * MAIN :] = rests[:MAIN]
            at = 2 * MAIN + f * REST
            wt[slot, at : at + REST, 2 * MAIN :] = rests[MAIN:]

    half = C // 2
    number = lax.broadcasted_iota(jnp.int32, (8, half), 1).astype(F32)
    which = lax.broadcasted_iota(jnp.int32, (8, half), 0)
    t = jnp.where(which == 0, timesteps[0], timesteps[1]).astype(F32)
    angle = t * jnp.exp(-math.log(10000.0) * number / half)
    emb = jnp.concatenate([jnp.cos(angle), jnp.sin(angle)], axis=1)
    bias = [
        jnp.dot(emb, raw_b[slot], preferred_element_type=F32, precision=lax.Precision.HIGHEST) for slot in range(2)
    ]

    def twice(value):
        return jnp.concatenate([value, value], axis=1)

    gain_main = [gains[slot : slot + 1, :MAIN] for slot in range(2)]
    gain_rest = [twice(gains[slot : slot + 1, MAIN:]) for slot in range(2)]
    two = jnp.full((1, 128), bounds[segment + 1] - bounds[segment], jnp.int32) > 1
    two_main = jnp.concatenate([two, two], axis=1)
    low = lanes((PIX, 128)) < REST

    for step in range(STEPS):
        bias_main = [bias[slot][step : step + 1, :MAIN] for slot in range(2)]
        bias_rest = [twice(bias[slot][step : step + 1, MAIN:]) for slot in range(2)]
        far, own, near = (arrived.at[step, at] for at in range(3))

        def keep(at, main_a, main_b, rest):
            hidden[at] = jnp.concatenate([main_a, main_b, rest], axis=1).astype(BF16)
            norm_pair(hidden[at], gain_main[1], gain_rest[1], hm, hr, 2 * at, 2 * at + 1, at)

        for part in parts:
            own_copy(step, part).wait_recv()
            inner_copy(step, part).start()

            @pl.when(has_across)
            def _(step=step, part=part):
                across_copy(step, part).start()

            begin, size = PARTS[part]
            spot = slice(begin, begin + size)
            norm_pair(own[spot], gain_main[0], gain_rest[0], xm, xr, 2, 3, 1, spot)
        for tile in range(4):
            zf[:, columns(tile)] = after_part(xm, 2, xr[1], wm.at[0], w_own.at[0], tile)

        for part in parts:
            inner_copy(step, part).wait_recv()
        norm_pair(near[...], gain_main[0], gain_rest[0], xm, xr, 5, 4, 2)
        rests = jnp.concatenate([xr[1], xr[2]], axis=1)
        centre = (second_of(own), second_of(near), jnp.where(low, roll_rest(rests_of(own)), rests_of(near)))
        results = finish(
            lambda tile: both_parts(xm, 2, rests, wm.at[0], w_near, tile), centre, wt.at[0], bias_main[0], bias_rest[0]
        )
        keep(1, *results)
        for tile in range(4):
            zh[:, columns(tile)] = after_part(hm, 2, hr[1], wm.at[1], w_own.at[1], tile)

        @pl.when(has_across)
        def _(step=step):
            for part in parts:
                across_copy(step, part).wait_recv()

        norm_pair(far[...], gain_main[0], gain_rest[0], xm, xr, 1, 0, 0)
        centre = (first_of(far), first_of(own), jnp.where(low, rests_of(far), roll_rest(rests_of(own))))
        main_a, main_b, rest = finish(
            lambda tile: zf[:, columns(tile)] + before_part(xm, 0, xr[0], wm.at[0], w_far, tile),
            centre, wt.at[0], bias_main[0], bias_rest[0],
        )
        keep(0, jnp.where(has_across, main_a, 0.0), main_b, jnp.where(low, jnp.where(has_across, rest, 0.0), rest))
        centre = (
            second_of(hidden.at[0]),
            first_of(hidden.at[1]),
            roll_rest(jnp.where(low, rests_of(hidden.at[1]), rests_of(hidden.at[0]))),
        )
        main_a, main_b, rest = finish(
            lambda tile: zh[:, columns(tile)] + before_part(hm, 0, hr[0], wm.at[1], w_hid, tile),
            centre, wt.at[1], bias_main[1], bias_rest[1],
        )
        main_a = jnp.where(two_main, main_a, centre[0])
        main_b = jnp.where(two_main, main_b, centre[1])
        rest = jnp.where(two, rest, centre[2])
        if step + 1 < STEPS:
            packed[step + 1] = jnp.concatenate([main_a, main_b, rest], axis=1).astype(BF16)
            for part in parts:
                own_copy(step + 1, part).start()
        else:
            out[...] = jnp.concatenate([main_a, main_b, rest], axis=1).astype(BF16)

    for step in range(STEPS):
        for part in parts:
            own_copy(step, part).wait_send()
            inner_copy(step, part).wait_send()

        @pl.when(has_across)
        def _(step=step):
            for part in parts:
                across_copy(step, part).wait_send()


def unpack(pair, out, strip, pixels):
    core = lax.rem(lax.axis_index("rows"), 2)
    low_half = lanes((W // 2, 128)) < REST
    rest = rests_of(pair)
    for at, (main, ends) in enumerate(((first_of(pair), rest), (second_of(pair), roll_rest(rest)))):
        pixels[at, 0], pixels[at, 1], pixels[at, 2] = main[:, :128], main[:, 128:], ends
    for f in range(FRAMES):
        for row, at in ((0, core), (1, 1 - core)):
            even, odd = (
                [pixels[at, k, pl.ds(f * W + one, W // 2, stride=2)] for k in range(3)] for one in range(2)
            )
            odd = [roll_rest(tile) for tile in odd]
            own = [even[0], even[1]]
            own += [jnp.where(low_half, one, two) for one, two in ((even[2], odd[0]), odd[:2], odd[1:])]
            for k in range(TILES):
                strip[f, k, pl.ds(row, W // 2, stride=2)] = own[k]
        for pair in range(W // 2):
            for k in range(TILES):
                begin = 2 * C * pair + 128 * k
                out[0, f, :, begin : begin + 128] = strip[f, k, 2 * pair : 2 * pair + 2].astype(BF16)


def body(state, bounds, timesteps, gains, spatial_weight, temporal_weight, time_weight):
    vmem = pl.BlockSpec(memory_space=pltpu.VMEM)
    smem = pl.BlockSpec(memory_space=pltpu.SMEM)
    hbm = pl.BlockSpec(memory_space=pl.ANY)
    pair = pl.pallas_call(
        kernel,
        out_shape=pltpu.VMEM((PIX, PACK), BF16),
        in_specs=[hbm, smem, smem, vmem, hbm, hbm, hbm],
        out_specs=vmem,
        scratch_shapes=[
            pltpu.VMEM((FRAMES, 2, W * C), BF16),
            pltpu.VMEM((FRAMES, TILES, W, 128), F32),
            pltpu.VMEM((2, 3, PIX, 128), F32),
            pltpu.VMEM((2, 9, C, C), BF16),
            pltpu.VMEM((2, 3, C, C), BF16),
            pltpu.VMEM((2, C, C), F32),
            pltpu.VMEM((2, 3 * MAIN, NOUT), BF16),
            pltpu.VMEM((2, 4 * REST, NOUT), BF16),
            pltpu.VMEM((2, 2, 2 * REST, NOUT), BF16),
            pltpu.VMEM((2, 2 * REST, NOUT), BF16),
            pltpu.VMEM((2, 2 * REST, NOUT), BF16),
            pltpu.VMEM((2, PACK, PACK), BF16),
            pltpu.VMEM((STEPS, PIX, PACK), BF16),
            pltpu.VMEM((STEPS, 3, PIX, PACK), BF16),
            pltpu.VMEM((2, PIX, PACK), BF16),
            pltpu.VMEM((6, PIX, MAIN), BF16),
            pltpu.VMEM((3, PIX, 128), BF16),
            pltpu.VMEM((4, PIX, MAIN), BF16),
            pltpu.VMEM((2, PIX, 128), BF16),
            pltpu.VMEM((2 * PIX, NOUT), F32),
            pltpu.VMEM((2 * PIX, NOUT), F32),
            pltpu.SemaphoreType.DMA((3, 3)),
            pltpu.SemaphoreType.DMA((STEPS, 3, len(PARTS))),
            pltpu.SemaphoreType.DMA((STEPS, 3, len(PARTS))),
        ],
        compiler_params=pltpu.CompilerParams(
            collective_id=1, has_side_effects=True, vmem_limit_bytes=56 << 20
        ),
        cost_estimate=pl.CostEstimate(flops=4 << 30, bytes_accessed=6 << 20, transcendentals=1 << 20),
        name="cycle",
    )(
        state,
        bounds,
        timesteps,
        gains.reshape(2, C),
        spatial_weight.reshape(2, 9, C, C),
        temporal_weight.reshape(2, 3, C, C),
        time_weight.reshape(2, C, C),
    )
    return pl.pallas_call(
        unpack,
        out_shape=jax.ShapeDtypeStruct((1, FRAMES, 2, W * C), BF16),
        in_specs=[vmem],
        out_specs=vmem,
        scratch_shapes=[pltpu.VMEM((FRAMES, TILES, W, 128), F32), pltpu.VMEM((2, 3, PIX, 128), F32)],
        compiler_params=pltpu.CompilerParams(vmem_limit_bytes=16 << 20),
        name="unpack",
    )(pair)


def solution(mesh):
    placed = (
        P("segment", None, "rows", None),
        P(),
        P(),
        P("segment", None, None),
        P("segment", None, None, None, None, None),
        P("segment", None, None, None, None),
        P("segment", None, None, None),
    )
    return jax.shard_map(
        body,
        mesh=mesh,
        in_specs=placed,
        out_specs=P("segment", None, "rows", None),
        check_vma=False,
    )
```

```python
import math

import jax
import jax.numpy as jnp
from jax import lax
from jax.experimental import pallas as pl
from jax.experimental.pallas import tpu as pltpu
from jax.sharding import PartitionSpec as P

C = 320
W = 72
STEPS = 2
FRAMES = 2
SEGMENTS = 4
GROUPS = 64
MAIN = 256
REST = C - MAIN
PIX = FRAMES * W
PACK = 2 * MAIN + 2 * REST
TILES = 2 * C // 128
NOUT = 3 * MAIN
NENDS = 3 * 128
PARTS = ((0, 32), (32, 32), (64, 32), (96, 32), (128, 16))
NEAR = ((0, 1, None, 2), (None, 0, 2, 1))
AFTER = ((2, None), (1, 2))
BEFORE = ((0, 1), (None, 0))
BEFORE_REVERSED = ((1, 0), (0, None))
MESH = pl.DeviceIdType.MESH
F32 = jnp.float32
BF16 = jnp.bfloat16


def lanes(shape):
    return lax.broadcasted_iota(jnp.int32, shape, len(shape) - 1)


def roll_rest(value):
    return pltpu.roll(value, REST, 1)


def norm_pair(pair, gain_main, gain_rest, xm, xr, first, second, at, spot=slice(None)):
    main_a = pair[:, :MAIN].astype(F32)
    main_b = pair[:, MAIN : 2 * MAIN].astype(F32)
    rest = pair[:, 2 * MAIN :].astype(F32)
    low = lanes(rest.shape) < REST
    square = rest * rest
    zero = jnp.zeros_like(square)

    def scale(main, own):
        both = main * main
        total = both[:, :128] + both[:, 128:] + own
        return lax.rsqrt(jnp.sum(total, axis=-1, keepdims=True) * (1.0 / C) + 1e-06)

    scale_a = scale(main_a, jnp.where(low, square, zero))
    scale_b = scale(main_b, jnp.where(low, zero, square))
    xm[first, spot] = (main_a * scale_a * gain_main).astype(BF16)
    xm[second, spot] = (main_b * scale_b * gain_main).astype(BF16)
    xr[at, spot] = (rest * jnp.where(low, scale_a, scale_b) * gain_rest).astype(BF16)


def first_of(pair):
    return pair[:, :MAIN].astype(F32)


def second_of(pair):
    return pair[:, MAIN : 2 * MAIN].astype(F32)


def rests_of(pair):
    return pair[:, 2 * MAIN :].astype(F32)


def dot(left, right):
    return jnp.dot(left, right, preferred_element_type=F32)


def columns(tile):
    return slice(tile * MAIN, (tile + 1) * MAIN)


def before_part(xm, row, rest, wm, wr, we, we_rest, tile, out_row):
    cols = columns(tile)
    both = jnp.concatenate([xm[row], xm[row + 1]], axis=1)
    if tile == 3:
        return dot(both, we[: 2 * MAIN]) + dot(rest, we_rest[...])
    if out_row == 0:
        return dot(both, wm[: 2 * MAIN, cols]) + dot(rest, wr[0, :, cols])
    return dot(xm[row + 1], wm[:MAIN, cols]) + dot(rest, wr[1, :, cols])


def after_part(xm, row, rest, wm, wr, we, we_rest, tile):
    cols = columns(tile)
    both = jnp.concatenate([xm[row], xm[row + 1]], axis=1)
    if tile == 3:
        return dot(both, we[2 * MAIN :]) + dot(rest, we_rest[...])
    one = dot(xm[row], wm[2 * MAIN :, cols]) + dot(rest, wr[0, :, cols])
    two = dot(both, wm[MAIN:, cols]) + dot(rest, wr[1, :, cols])
    return jnp.concatenate([one, two], axis=0)


def both_parts(xm, row, rest, wm, wr, we, we_rest, tile):
    cols = columns(tile)
    if tile == 3:
        return dot(jnp.concatenate([xm[row + at] for at in range(4)], axis=1), we[...]) + dot(rest, we_rest[...])
    left = jnp.concatenate([xm[row + dy : row + dy + 2].reshape(2 * PIX, MAIN) for dy in range(3)], axis=1)
    rests = jnp.concatenate([dot(rest, wr[0, :, cols]), dot(rest, wr[1, :, cols])], axis=0)
    return dot(left, wm[:, cols]) + rests


def finish(product, centre, wt, bias_main, bias_rest):
    wt_main, wt_rest, wt_ends = wt

    def from_before(value):
        spot = lax.rem(lax.broadcasted_iota(jnp.int32, (value.shape[0], 1), 0), W)
        return jnp.where(spot == 0, 0.0, pltpu.roll(value, 1, 0))

    def from_after(value):
        spot = lax.rem(lax.broadcasted_iota(jnp.int32, (value.shape[0], 1), 0), W)
        return jnp.where(spot == W - 1, 0.0, pltpu.roll(value, value.shape[0] - 1, 0))

    def silu(value):
        return value * (0.5 * jnp.tanh(0.5 * value) + 0.5)

    z = product(3, None)
    a_rest = from_before(z[:, :128]) + z[:, 128:256] + from_after(z[:, 256:]) + bias_rest
    u_rest = silu(a_rest)
    a_main, lines = [], []
    for row in range(2):
        taps = [product(tile, row) for tile in range(3)]
        a_main.append(from_before(taps[0]) + taps[1] + from_after(taps[2]) + bias_main)
        u_main = silu(a_main[row])
        lines.append([u_main[:W], u_main[W:]])
    mixed = jnp.concatenate([jnp.concatenate([lines[row][f] for row in range(2)], axis=0) for f in range(FRAMES)], axis=1)
    mixed = mixed.astype(BF16)
    ends = jnp.concatenate([u_rest[:W], u_rest[W:]], axis=1).astype(BF16)
    wide = jnp.concatenate([lines[row][f] for row in range(2) for f in range(FRAMES)], axis=1).astype(BF16)
    v_rest = dot(wide, wt_ends[: 4 * MAIN]) + dot(ends, wt_ends[4 * MAIN :])
    v = dot(mixed, wt_main[...])
    v_rows = []
    for row in range(2):
        own = v[row * W : (row + 1) * W] + dot(ends, wt_rest[row])
        v_rows.append(jnp.concatenate([own[:, :MAIN], own[:, MAIN:]], axis=0))
    v_rest = jnp.concatenate([v_rest[:, :128], v_rest[:, 128:]], axis=0)
    h_a, h_b, h_rest = centre
    return h_a + a_main[0] + v_rows[0], h_b + a_main[1] + v_rows[1], h_rest + a_rest + v_rest


def kernel(
    state, bounds, timesteps, gains, spatial, temporal, time_weight,
    out,
    raw_x, strip, pixels, raw_s, raw_t, raw_b, wm, w_near, w_own, w_far, w_hid, we, e_near, e_own, e_far, e_hid, wt_main, wt_rest, wt_ends,
    packed, arrived, hidden, xm, xr, hm, hr, zf, zh, zfe, zhe,
    load_sem, send_sem, recv_sem,
):
    segment = lax.axis_index("segment")
    group = lax.axis_index("rows")
    core = lax.rem(group, 2)
    behind, ahead = lax.rem(segment + SEGMENTS - 1, SEGMENTS), lax.rem(segment + 1, SEGMENTS)
    across = group - 1 + 2 * core
    inner = group + 1 - 2 * core
    has_across = (across >= 0) & (across < GROUPS)

    loads = []
    for slot in range(2):
        loads.append(
            (
                pltpu.make_async_copy(spatial.at[slot], raw_s.at[slot], load_sem.at[slot, 0]),
                pltpu.make_async_copy(temporal.at[slot], raw_t.at[slot], load_sem.at[slot, 1]),
                pltpu.make_async_copy(time_weight.at[slot], raw_b.at[slot], load_sem.at[slot, 2]),
            )
        )

    barrier = pltpu.get_barrier_semaphore()
    pl.semaphore_signal(barrier, inc=1, device_id=(behind, group), device_id_type=MESH)
    pl.semaphore_signal(barrier, inc=1, device_id=(segment, inner), device_id_type=MESH)

    @pl.when(has_across)
    def _():
        pl.semaphore_signal(barrier, inc=1, device_id=(segment, across), device_id_type=MESH)

    state_load = pltpu.make_async_copy(state.at[0], raw_x, load_sem.at[2, 0])
    for load in (state_load, *loads[0], *loads[1]):
        load.start()

    state_load.wait()
    low_half = lanes((W // 2, 128)) < REST
    for f in range(FRAMES):
        for pair in range(W // 2):
            for k in range(TILES):
                begin = 2 * C * pair + 128 * k
                strip[f, k, 2 * pair : 2 * pair + 2] = raw_x[f, :, begin : begin + 128].astype(F32)
        for row, at in ((0, core), (1, 1 - core)):
            own = [strip[f, k, pl.ds(row, W // 2, stride=2)] for k in range(TILES)]
            swapped = [None, None] + [roll_rest(tile) for tile in own[2:]]
            odd = [jnp.where(low_half, swapped[2 + k], swapped[min(3 + k, 4)]) for k in range(3)]
            for k in range(3):
                pixels[at, k, pl.ds(f * W, W // 2, stride=2)] = own[k]
                pixels[at, k, pl.ds(f * W + 1, W // 2, stride=2)] = odd[k]
    rest = jnp.where(lanes((PIX, 128)) < REST, pixels[0, 2], roll_rest(pixels[1, 2]))
    packed[0] = jnp.concatenate([pixels[at, k] for at in range(2) for k in range(2)] + [rest], axis=1).astype(BF16)

    pl.semaphore_wait(barrier, 2 + has_across.astype(jnp.int32))

    def piece(step, kind, part, source, target, device):
        spot = pl.ds(*PARTS[part])
        return pltpu.make_async_remote_copy(
            source.at[spot], target.at[spot], send_sem.at[step, kind, part], recv_sem.at[step, kind, part],
            device_id=device, device_id_type=MESH,
        )

    def own_copy(step, part):
        return piece(step, 0, part, packed.at[step], arrived.at[step, 1], (ahead, group))

    def across_copy(step, part):
        return piece(step, 1, part, arrived.at[step, 1], arrived.at[step, 0], (segment, across))

    def inner_copy(step, part):
        return piece(step, 2, part, arrived.at[step, 1], arrived.at[step, 2], (segment, inner))

    parts = range(len(PARTS))
    for part in parts:
        own_copy(0, part).start()

    @pl.when(jnp.logical_not(has_across))
    def _():
        for step in range(STEPS):
            arrived[step, 0] = jnp.zeros((PIX, PACK), BF16)

    none = jnp.zeros((REST, NOUT), BF16)
    wt = [(wt_main.at[slot], wt_rest.at[slot], wt_ends.at[slot]) for slot in range(2)]
    for slot in range(2):
        for load in loads[slot]:
            load.wait()
        for dy in range(3):
            taps = [3 * (dy + core * (2 - 2 * dy)) + dx for dx in range(3)]
            for dx in range(3):
                wm[slot, dy * MAIN : (dy + 1) * MAIN, columns(dx)] = raw_s[slot, taps[dx], :MAIN, :MAIN]
            tail = jnp.concatenate([raw_s[slot, tap, MAIN:, :MAIN] for tap in taps], axis=1)
            if slot == 0:
                places = ((w_near, NEAR), (w_own.at[slot], AFTER), (w_far, BEFORE_REVERSED))
            else:
                places = ((w_own.at[slot], AFTER), (w_hid, BEFORE))
            for ref, order in places:
                for row in range(2):
                    for at, tap in enumerate(order[row]):
                        if tap == dy:
                            ref[row, at * REST : (at + 1) * REST] = tail
                        elif tap is None and dy == 0:
                            ref[row, at * REST : (at + 1) * REST] = none
        blank = jnp.zeros((C, REST), BF16)

        def ends_of(i):
            tap = lambda dy, dx: raw_s[slot, 3 * (dy + core * (2 - 2 * dy)) + dx, :, MAIN:] if 0 <= dy < 3 else blank
            return jnp.concatenate([tap(i - row, dx) for dx in range(3) for row in range(2)], axis=1)

        ends = [ends_of(i) for i in range(4)]
        for i in range(4):
            we[slot, i * MAIN : (i + 1) * MAIN] = ends[i][:MAIN]
        places = ((e_near, (0, 1, 3, 2)), (e_own.at[slot], (2, 3)), (e_far, (1, 0)))
        for ref, order in places if slot == 0 else ((e_own.at[slot], (2, 3)), (e_hid, (0, 1))):
            for at, i in enumerate(order):
                ref[at * REST : (at + 1) * REST] = ends[i][MAIN:]
        nil = jnp.zeros((REST, FRAMES * MAIN), BF16)
        blank = jnp.zeros((C, REST), BF16)
        for f in range(FRAMES):
            taps = [f - g + 1 for g in range(FRAMES)]
            for g in range(FRAMES):
                wt_main[slot, f * MAIN : (f + 1) * MAIN, columns(g)] = raw_t[slot, taps[g], :MAIN, :MAIN]
            tail = jnp.concatenate([raw_t[slot, tap, MAIN:, :MAIN] for tap in taps], axis=1)
            for row in range(2):
                for at in range(2):
                    begin = (2 * f + at) * REST
                    wt_rest[slot, row, begin : begin + REST] = tail if at == row else nil
                ends = [raw_t[slot, tap, :, MAIN:] for tap in taps]
                ends = jnp.concatenate([ends[g] if at == row else blank for g in range(FRAMES) for at in range(2)], axis=1)
                wt_ends[slot, (2 * row + f) * MAIN : (2 * row + f + 1) * MAIN] = ends[:MAIN]
                begin = 4 * MAIN + (2 * f + row) * REST
                wt_ends[slot, begin : begin + REST] = ends[MAIN:]

    half = C // 2
    number = lax.broadcasted_iota(jnp.int32, (8, half), 1).astype(F32)
    which = lax.broadcasted_iota(jnp.int32, (8, half), 0)
    t = jnp.where(which == 0, timesteps[0], timesteps[1]).astype(F32)
    angle = t * jnp.exp(-math.log(10000.0) * number / half)
    emb = jnp.concatenate([jnp.cos(angle), jnp.sin(angle)], axis=1)
    bias = [
        jnp.dot(emb, raw_b[slot], preferred_element_type=F32, precision=lax.Precision.HIGHEST) for slot in range(2)
    ]

    def twice(value):
        return jnp.concatenate([value, value], axis=1)

    gain_main = [gains[slot : slot + 1, :MAIN] for slot in range(2)]
    gain_rest = [twice(gains[slot : slot + 1, MAIN:]) for slot in range(2)]
    two = jnp.full((1, 128), bounds[segment + 1] - bounds[segment], jnp.int32) > 1
    two_main = jnp.concatenate([two, two], axis=1)
    low = lanes((PIX, 128)) < REST

    for step in range(STEPS):
        bias_main = [bias[slot][step : step + 1, :MAIN] for slot in range(2)]
        bias_rest = [twice(bias[slot][step : step + 1, MAIN:]) for slot in range(2)]
        far, own, near = (arrived.at[step, at] for at in range(3))

        def keep(at, main_a, main_b, rest):
            hidden[at] = jnp.concatenate([main_a, main_b, rest], axis=1).astype(BF16)
            norm_pair(hidden[at], gain_main[1], gain_rest[1], hm, hr, 2 * at, 2 * at + 1, at)

        for part in parts:
            own_copy(step, part).wait_recv()
            inner_copy(step, part).start()

            @pl.when(has_across)
            def _(step=step, part=part):
                across_copy(step, part).start()

            begin, size = PARTS[part]
            spot = slice(begin, begin + size)
            norm_pair(own[spot], gain_main[0], gain_rest[0], xm, xr, 2, 3, 1, spot)
        for tile in range(4):
            part = after_part(xm, 2, xr[1], wm.at[0], w_own.at[0], we.at[0], e_own.at[0], tile)
            if tile == 3:
                zfe[...] = part
            else:
                zf[:, columns(tile)] = part

        for part in parts:
            inner_copy(step, part).wait_recv()
        norm_pair(near[...], gain_main[0], gain_rest[0], xm, xr, 5, 4, 2)
        rests = jnp.concatenate([xr[1], xr[2]], axis=1)
        own_turned = roll_rest(rests_of(own))
        centre = (second_of(own), second_of(near), jnp.where(low, own_turned, rests_of(near)))
        products = [both_parts(xm, 2, rests, wm.at[0], w_near, we.at[0], e_near, tile) for tile in range(4)]
        results = finish(
            lambda tile, row: products[tile] if row is None else products[tile][row * PIX : (row + 1) * PIX],
            centre, wt[0], bias_main[0], bias_rest[0],
        )
        keep(1, *results)
        for tile in range(4):
            part = after_part(hm, 2, hr[1], wm.at[1], w_own.at[1], we.at[1], e_own.at[1], tile)
            if tile == 3:
                zhe[...] = part
            else:
                zh[:, columns(tile)] = part

        def early(z, ends, tile, row):
            return ends[...] if row is None else z[row * PIX : (row + 1) * PIX, columns(tile)]

        @pl.when(has_across)
        def _(step=step):
            for part in parts:
                across_copy(step, part).wait_recv()

        norm_pair(far[...], gain_main[0], gain_rest[0], xm, xr, 1, 0, 0)
        centre = (first_of(far), first_of(own), jnp.where(low, rests_of(far), own_turned))
        main_a, main_b, rest = finish(
            lambda tile, row: early(zf, zfe, tile, row) + before_part(xm, 0, xr[0], wm.at[0], w_far, we.at[0], e_far, tile, row),
            centre, wt[0], bias_main[0], bias_rest[0],
        )
        keep(0, jnp.where(has_across, main_a, 0.0), main_b, jnp.where(low, jnp.where(has_across, rest, 0.0), rest))
        centre = (
            second_of(hidden.at[0]),
            first_of(hidden.at[1]),
            roll_rest(jnp.where(low, rests_of(hidden.at[1]), rests_of(hidden.at[0]))),
        )
        main_a, main_b, rest = finish(
            lambda tile, row: early(zh, zhe, tile, row) + before_part(hm, 0, hr[0], wm.at[1], w_hid, we.at[1], e_hid, tile, row),
            centre, wt[1], bias_main[1], bias_rest[1],
        )
        main_a = jnp.where(two_main, main_a, centre[0])
        main_b = jnp.where(two_main, main_b, centre[1])
        rest = jnp.where(two, rest, centre[2])
        if step + 1 < STEPS:
            packed[step + 1] = jnp.concatenate([main_a, main_b, rest], axis=1).astype(BF16)
            for part in parts:
                own_copy(step + 1, part).start()
        else:
            out[...] = jnp.concatenate([main_a, main_b, rest], axis=1).astype(BF16)

    for step in range(STEPS):
        for part in parts:
            own_copy(step, part).wait_send()
            inner_copy(step, part).wait_send()

        @pl.when(has_across)
        def _(step=step):
            for part in parts:
                across_copy(step, part).wait_send()


def unpack(pair, out, strip, pixels):
    core = lax.rem(lax.axis_index("rows"), 2)
    low_half = lanes((W // 2, 128)) < REST
    rest = rests_of(pair)
    for at, (main, ends) in enumerate(((first_of(pair), rest), (second_of(pair), roll_rest(rest)))):
        pixels[at, 0], pixels[at, 1], pixels[at, 2] = main[:, :128], main[:, 128:], ends
    for f in range(FRAMES):
        for row, at in ((0, core), (1, 1 - core)):
            even, odd = (
                [pixels[at, k, pl.ds(f * W + one, W // 2, stride=2)] for k in range(3)] for one in range(2)
            )
            odd = [roll_rest(tile) for tile in odd]
            own = [even[0], even[1]]
            own += [jnp.where(low_half, one, two) for one, two in ((even[2], odd[0]), odd[:2], odd[1:])]
            for k in range(TILES):
                strip[f, k, pl.ds(row, W // 2, stride=2)] = own[k]
        for pair in range(W // 2):
            for k in range(TILES):
                begin = 2 * C * pair + 128 * k
                out[0, f, :, begin : begin + 128] = strip[f, k, 2 * pair : 2 * pair + 2].astype(BF16)


def body(state, bounds, timesteps, gains, spatial_weight, temporal_weight, time_weight):
    vmem = pl.BlockSpec(memory_space=pltpu.VMEM)
    smem = pl.BlockSpec(memory_space=pltpu.SMEM)
    hbm = pl.BlockSpec(memory_space=pl.ANY)
    pair = pl.pallas_call(
        kernel,
        out_shape=pltpu.VMEM((PIX, PACK), BF16),
        in_specs=[hbm, smem, smem, vmem, hbm, hbm, hbm],
        out_specs=vmem,
        scratch_shapes=[
            pltpu.VMEM((FRAMES, 2, W * C), BF16),
            pltpu.VMEM((FRAMES, TILES, W, 128), F32),
            pltpu.VMEM((2, 3, PIX, 128), F32),
            pltpu.VMEM((2, 9, C, C), BF16),
            pltpu.VMEM((2, 3, C, C), BF16),
            pltpu.VMEM((2, C, C), F32),
            pltpu.VMEM((2, 3 * MAIN, NOUT), BF16),
            pltpu.VMEM((2, 4 * REST, NOUT), BF16),
            pltpu.VMEM((2, 2, 2 * REST, NOUT), BF16),
            pltpu.VMEM((2, 2 * REST, NOUT), BF16),
            pltpu.VMEM((2, 2 * REST, NOUT), BF16),
            pltpu.VMEM((2, 4 * MAIN, NENDS), BF16),
            pltpu.VMEM((4 * REST, NENDS), BF16),
            pltpu.VMEM((2, 2 * REST, NENDS), BF16),
            pltpu.VMEM((2 * REST, NENDS), BF16),
            pltpu.VMEM((2 * REST, NENDS), BF16),
            pltpu.VMEM((2, 2 * MAIN, 2 * MAIN), BF16),
            pltpu.VMEM((2, 2, 4 * REST, 2 * MAIN), BF16),
            pltpu.VMEM((2, 4 * MAIN + 4 * REST, 4 * REST), BF16),
            pltpu.VMEM((STEPS, PIX, PACK), BF16),
            pltpu.VMEM((STEPS, 3, PIX, PACK), BF16),
            pltpu.VMEM((2, PIX, PACK), BF16),
            pltpu.VMEM((6, PIX, MAIN), BF16),
            pltpu.VMEM((3, PIX, 128), BF16),
            pltpu.VMEM((4, PIX, MAIN), BF16),
            pltpu.VMEM((2, PIX, 128), BF16),
            pltpu.VMEM((2 * PIX, NOUT), F32),
            pltpu.VMEM((2 * PIX, NOUT), F32),
            pltpu.VMEM((PIX, NENDS), F32),
            pltpu.VMEM((PIX, NENDS), F32),
            pltpu.SemaphoreType.DMA((3, 3)),
            pltpu.SemaphoreType.DMA((STEPS, 3, len(PARTS))),
            pltpu.SemaphoreType.DMA((STEPS, 3, len(PARTS))),
        ],
        compiler_params=pltpu.CompilerParams(
            collective_id=1, has_side_effects=True, vmem_limit_bytes=56 << 20
        ),
        cost_estimate=pl.CostEstimate(flops=4 << 30, bytes_accessed=6 << 20, transcendentals=1 << 20),
        name="cycle",
    )(
        state,
        bounds,
        timesteps,
        gains.reshape(2, C),
        spatial_weight.reshape(2, 9, C, C),
        temporal_weight.reshape(2, 3, C, C),
        time_weight.reshape(2, C, C),
    )
    return pl.pallas_call(
        unpack,
        out_shape=jax.ShapeDtypeStruct((1, FRAMES, 2, W * C), BF16),
        in_specs=[vmem],
        out_specs=vmem,
        scratch_shapes=[pltpu.VMEM((FRAMES, TILES, W, 128), F32), pltpu.VMEM((2, 3, PIX, 128), F32)],
        compiler_params=pltpu.CompilerParams(vmem_limit_bytes=16 << 20),
        name="unpack",
    )(pair)


def solution(mesh):
    placed = (
        P("segment", None, "rows", None),
        P(),
        P(),
        P("segment", None, None),
        P("segment", None, None, None, None, None),
        P("segment", None, None, None, None),
        P("segment", None, None, None),
    )
    return jax.shard_map(
        body,
        mesh=mesh,
        in_specs=placed,
        out_specs=P("segment", None, "rows", None),
        check_vma=False,
    )
```

```python
import math

import jax
import jax.numpy as jnp
from jax import lax
from jax.experimental import pallas as pl
from jax.experimental.pallas import tpu as pltpu
from jax.sharding import PartitionSpec as P

C = 320
W = 72
STEPS = 2
CHAIN = 8
FRAMES = 2
SEGMENTS = 4
GROUPS = 64
MAIN = 256
REST = C - MAIN
PIX = FRAMES * W
PACK = 2 * MAIN + 2 * REST
TILES = 2 * C // 128
NOUT = 3 * MAIN
NENDS = 3 * 128
PARTS = ((0, 32), (32, 32), (64, 32), (96, 32), (128, 16))
NEAR = ((0, 1, None, 2), (None, 0, 2, 1))
AFTER = ((2, None), (1, 2))
BEFORE = ((0, 1), (None, 0))
BEFORE_REVERSED = ((1, 0), (0, None))
MESH = pl.DeviceIdType.MESH
F32 = jnp.float32
BF16 = jnp.bfloat16


def lanes(shape):
    return lax.broadcasted_iota(jnp.int32, shape, len(shape) - 1)


def roll_rest(value):
    return pltpu.roll(value, REST, 1)


def norm_pair(pair, gain_main, gain_rest, xm, xr, first, second, at, spot=slice(None)):
    main_a = pair[:, :MAIN].astype(F32)
    main_b = pair[:, MAIN : 2 * MAIN].astype(F32)
    rest = pair[:, 2 * MAIN :].astype(F32)
    low = lanes(rest.shape) < REST
    square = rest * rest
    zero = jnp.zeros_like(square)

    def scale(main, own):
        both = main * main
        total = both[:, :128] + both[:, 128:] + own
        return lax.rsqrt(jnp.sum(total, axis=-1, keepdims=True) * (1.0 / C) + 1e-06)

    scale_a = scale(main_a, jnp.where(low, square, zero))
    scale_b = scale(main_b, jnp.where(low, zero, square))
    xm[first, spot] = (main_a * scale_a * gain_main).astype(BF16)
    xm[second, spot] = (main_b * scale_b * gain_main).astype(BF16)
    xr[at, spot] = (rest * jnp.where(low, scale_a, scale_b) * gain_rest).astype(BF16)


def first_of(pair):
    return pair[:, :MAIN].astype(F32)


def second_of(pair):
    return pair[:, MAIN : 2 * MAIN].astype(F32)


def rests_of(pair):
    return pair[:, 2 * MAIN :].astype(F32)


def dot(left, right):
    return jnp.dot(left, right, preferred_element_type=F32)


def columns(tile):
    return slice(tile * MAIN, (tile + 1) * MAIN)


def before_part(xm, row, rest, wm, wr, we, we_rest, tile, out_row):
    cols = columns(tile)
    both = jnp.concatenate([xm[row], xm[row + 1]], axis=1)
    if tile == 3:
        return dot(both, we[: 2 * MAIN]) + dot(rest, we_rest[...])
    if out_row == 0:
        return dot(both, wm[: 2 * MAIN, cols]) + dot(rest, wr[0, :, cols])
    return dot(xm[row + 1], wm[:MAIN, cols]) + dot(rest, wr[1, :, cols])


def after_part(xm, row, rest, wm, wr, we, we_rest, tile):
    cols = columns(tile)
    both = jnp.concatenate([xm[row], xm[row + 1]], axis=1)
    if tile == 3:
        return dot(both, we[2 * MAIN :]) + dot(rest, we_rest[...])
    one = dot(xm[row], wm[2 * MAIN :, cols]) + dot(rest, wr[0, :, cols])
    two = dot(both, wm[MAIN:, cols]) + dot(rest, wr[1, :, cols])
    return jnp.concatenate([one, two], axis=0)


def both_parts(xm, row, rest, wm, wr, we, we_rest, tile):
    cols = columns(tile)
    if tile == 3:
        return dot(jnp.concatenate([xm[row + at] for at in range(4)], axis=1), we[...]) + dot(rest, we_rest[...])
    left = jnp.concatenate([xm[row + dy : row + dy + 2].reshape(2 * PIX, MAIN) for dy in range(3)], axis=1)
    rests = jnp.concatenate([dot(rest, wr[0, :, cols]), dot(rest, wr[1, :, cols])], axis=0)
    return dot(left, wm[:, cols]) + rests


def finish(product, centre, wt, bias_main, bias_rest):
    wt_main, wt_rest, wt_ends = wt

    def from_before(value):
        spot = lax.rem(lax.broadcasted_iota(jnp.int32, (value.shape[0], 1), 0), W)
        return jnp.where(spot == 0, 0.0, pltpu.roll(value, 1, 0))

    def from_after(value):
        spot = lax.rem(lax.broadcasted_iota(jnp.int32, (value.shape[0], 1), 0), W)
        return jnp.where(spot == W - 1, 0.0, pltpu.roll(value, value.shape[0] - 1, 0))

    def silu(value):
        return value * (0.5 * jnp.tanh(0.5 * value) + 0.5)

    z = product(3, None)
    a_rest = from_before(z[:, :128]) + z[:, 128:256] + from_after(z[:, 256:]) + bias_rest
    u_rest = silu(a_rest)
    a_main, lines = [], []
    for row in range(2):
        taps = [product(tile, row) for tile in range(3)]
        a_main.append(from_before(taps[0]) + taps[1] + from_after(taps[2]) + bias_main)
        u_main = silu(a_main[row])
        lines.append([u_main[:W], u_main[W:]])
    mixed = jnp.concatenate([jnp.concatenate([lines[row][f] for row in range(2)], axis=0) for f in range(FRAMES)], axis=1)
    mixed = mixed.astype(BF16)
    ends = jnp.concatenate([u_rest[:W], u_rest[W:]], axis=1).astype(BF16)
    wide = jnp.concatenate([lines[row][f] for row in range(2) for f in range(FRAMES)], axis=1).astype(BF16)
    v_rest = dot(wide, wt_ends[: 4 * MAIN]) + dot(ends, wt_ends[4 * MAIN :])
    v = dot(mixed, wt_main[...])
    v_rows = []
    for row in range(2):
        own = v[row * W : (row + 1) * W] + dot(ends, wt_rest[row])
        v_rows.append(jnp.concatenate([own[:, :MAIN], own[:, MAIN:]], axis=0))
    v_rest = jnp.concatenate([v_rest[:, :128], v_rest[:, 128:]], axis=0)
    h_a, h_b, h_rest = centre
    return h_a + a_main[0] + v_rows[0], h_b + a_main[1] + v_rows[1], h_rest + a_rest + v_rest


def kernel(
    state, bounds, timesteps, gains, spatial, temporal, time_weight,
    out,
    raw_x, strip, pixels, raw_s, raw_t, raw_b, wm, w_near, w_own, w_far, w_hid, we, e_near, e_own, e_far, e_hid, wt_main, wt_rest, wt_ends,
    packed, arrived, hidden, xm, xr, hm, hr, zf, zh, zfe, zhe,
    load_sem, send_sem, recv_sem, go_sem,
):
    segment = lax.axis_index("segment")
    group = lax.axis_index("rows")
    core = lax.rem(group, 2)
    behind, ahead = lax.rem(segment + SEGMENTS - 1, SEGMENTS), lax.rem(segment + 1, SEGMENTS)
    across = group - 1 + 2 * core
    inner = group + 1 - 2 * core
    has_across = (across >= 0) & (across < GROUPS)
    edge = lax.rem(group, CHAIN)
    goes_first = has_across & (edge == 0)
    goes_after = (edge == 1) & (group > 1)

    loads = []
    for slot in range(2):
        loads.append(
            (
                pltpu.make_async_copy(spatial.at[slot], raw_s.at[slot], load_sem.at[slot, 0]),
                pltpu.make_async_copy(temporal.at[slot], raw_t.at[slot], load_sem.at[slot, 1]),
                pltpu.make_async_copy(time_weight.at[slot], raw_b.at[slot], load_sem.at[slot, 2]),
            )
        )

    barrier = pltpu.get_barrier_semaphore()
    pl.semaphore_signal(barrier, inc=1, device_id=(behind, group), device_id_type=MESH)
    pl.semaphore_signal(barrier, inc=1, device_id=(segment, inner), device_id_type=MESH)

    @pl.when(has_across)
    def _():
        pl.semaphore_signal(barrier, inc=1, device_id=(segment, across), device_id_type=MESH)

    state_load = pltpu.make_async_copy(state.at[0], raw_x, load_sem.at[2, 0])
    for load in (state_load, *loads[0], *loads[1]):
        load.start()

    state_load.wait()
    low_half = lanes((W // 2, 128)) < REST
    for f in range(FRAMES):
        for pair in range(W // 2):
            for k in range(TILES):
                begin = 2 * C * pair + 128 * k
                strip[f, k, 2 * pair : 2 * pair + 2] = raw_x[f, :, begin : begin + 128].astype(F32)
        for row, at in ((0, core), (1, 1 - core)):
            own = [strip[f, k, pl.ds(row, W // 2, stride=2)] for k in range(TILES)]
            swapped = [None, None] + [roll_rest(tile) for tile in own[2:]]
            odd = [jnp.where(low_half, swapped[2 + k], swapped[min(3 + k, 4)]) for k in range(3)]
            for k in range(3):
                pixels[at, k, pl.ds(f * W, W // 2, stride=2)] = own[k]
                pixels[at, k, pl.ds(f * W + 1, W // 2, stride=2)] = odd[k]
    rest = jnp.where(lanes((PIX, 128)) < REST, pixels[0, 2], roll_rest(pixels[1, 2]))
    packed[0] = jnp.concatenate([pixels[at, k] for at in range(2) for k in range(2)] + [rest], axis=1).astype(BF16)

    pl.semaphore_wait(barrier, 2 + has_across.astype(jnp.int32))

    def piece(step, kind, part, source, target, device):
        spot = pl.ds(*PARTS[part])
        return pltpu.make_async_remote_copy(
            source.at[spot], target.at[spot], send_sem.at[step, kind, part], recv_sem.at[step, kind, part],
            device_id=device, device_id_type=MESH,
        )

    def own_copy(step, part):
        return piece(step, 0, part, packed.at[step], arrived.at[step, 1], (ahead, group))

    def across_copy(step, part):
        return piece(step, 1, part, arrived.at[step, 1], arrived.at[step, 0], (segment, across))

    def inner_copy(step, part):
        return piece(step, 2, part, arrived.at[step, 1], arrived.at[step, 2], (segment, inner))

    parts = range(len(PARTS))

    def send(step):
        @pl.when(goes_after)
        def _():
            pl.semaphore_wait(go_sem.at[step], 1)

        for part in parts:
            own_copy(step, part).start()

        @pl.when(goes_first)
        def _():
            for part in range(1):
                own_copy(step, part).wait_send()
            pl.semaphore_signal(go_sem.at[step], inc=1, device_id=(segment, inner), device_id_type=MESH)

    send(0)

    @pl.when(jnp.logical_not(has_across))
    def _():
        for step in range(STEPS):
            arrived[step, 0] = jnp.zeros((PIX, PACK), BF16)

    none = jnp.zeros((REST, NOUT), BF16)
    wt = [(wt_main.at[slot], wt_rest.at[slot], wt_ends.at[slot]) for slot in range(2)]
    for slot in range(2):
        for load in loads[slot]:
            load.wait()
        for dy in range(3):
            taps = [3 * (dy + core * (2 - 2 * dy)) + dx for dx in range(3)]
            for dx in range(3):
                wm[slot, dy * MAIN : (dy + 1) * MAIN, columns(dx)] = raw_s[slot, taps[dx], :MAIN, :MAIN]
            tail = jnp.concatenate([raw_s[slot, tap, MAIN:, :MAIN] for tap in taps], axis=1)
            if slot == 0:
                places = ((w_near, NEAR), (w_own.at[slot], AFTER), (w_far, BEFORE_REVERSED))
            else:
                places = ((w_own.at[slot], AFTER), (w_hid, BEFORE))
            for ref, order in places:
                for row in range(2):
                    for at, tap in enumerate(order[row]):
                        if tap == dy:
                            ref[row, at * REST : (at + 1) * REST] = tail
                        elif tap is None and dy == 0:
                            ref[row, at * REST : (at + 1) * REST] = none
        blank = jnp.zeros((C, REST), BF16)

        def ends_of(i):
            tap = lambda dy, dx: raw_s[slot, 3 * (dy + core * (2 - 2 * dy)) + dx, :, MAIN:] if 0 <= dy < 3 else blank
            return jnp.concatenate([tap(i - row, dx) for dx in range(3) for row in range(2)], axis=1)

        ends = [ends_of(i) for i in range(4)]
        for i in range(4):
            we[slot, i * MAIN : (i + 1) * MAIN] = ends[i][:MAIN]
        places = ((e_near, (0, 1, 3, 2)), (e_own.at[slot], (2, 3)), (e_far, (1, 0)))
        for ref, order in places if slot == 0 else ((e_own.at[slot], (2, 3)), (e_hid, (0, 1))):
            for at, i in enumerate(order):
                ref[at * REST : (at + 1) * REST] = ends[i][MAIN:]
        nil = jnp.zeros((REST, FRAMES * MAIN), BF16)
        blank = jnp.zeros((C, REST), BF16)
        for f in range(FRAMES):
            taps = [f - g + 1 for g in range(FRAMES)]
            for g in range(FRAMES):
                wt_main[slot, f * MAIN : (f + 1) * MAIN, columns(g)] = raw_t[slot, taps[g], :MAIN, :MAIN]
            tail = jnp.concatenate([raw_t[slot, tap, MAIN:, :MAIN] for tap in taps], axis=1)
            for row in range(2):
                for at in range(2):
                    begin = (2 * f + at) * REST
                    wt_rest[slot, row, begin : begin + REST] = tail if at == row else nil
                ends = [raw_t[slot, tap, :, MAIN:] for tap in taps]
                ends = jnp.concatenate([ends[g] if at == row else blank for g in range(FRAMES) for at in range(2)], axis=1)
                wt_ends[slot, (2 * row + f) * MAIN : (2 * row + f + 1) * MAIN] = ends[:MAIN]
                begin = 4 * MAIN + (2 * f + row) * REST
                wt_ends[slot, begin : begin + REST] = ends[MAIN:]

    half = C // 2
    number = lax.broadcasted_iota(jnp.int32, (8, half), 1).astype(F32)
    which = lax.broadcasted_iota(jnp.int32, (8, half), 0)
    t = jnp.where(which == 0, timesteps[0], timesteps[1]).astype(F32)
    angle = t * jnp.exp(-math.log(10000.0) * number / half)
    emb = jnp.concatenate([jnp.cos(angle), jnp.sin(angle)], axis=1)
    bias = [
        jnp.dot(emb, raw_b[slot], preferred_element_type=F32, precision=lax.Precision.HIGHEST) for slot in range(2)
    ]

    def twice(value):
        return jnp.concatenate([value, value], axis=1)

    gain_main = [gains[slot : slot + 1, :MAIN] for slot in range(2)]
    gain_rest = [twice(gains[slot : slot + 1, MAIN:]) for slot in range(2)]
    two = jnp.full((1, 128), bounds[segment + 1] - bounds[segment], jnp.int32) > 1
    two_main = jnp.concatenate([two, two], axis=1)
    low = lanes((PIX, 128)) < REST

    for step in range(STEPS):
        bias_main = [bias[slot][step : step + 1, :MAIN] for slot in range(2)]
        bias_rest = [twice(bias[slot][step : step + 1, MAIN:]) for slot in range(2)]
        far, own, near = (arrived.at[step, at] for at in range(3))

        def keep(at, main_a, main_b, rest):
            hidden[at] = jnp.concatenate([main_a, main_b, rest], axis=1).astype(BF16)
            norm_pair(hidden[at], gain_main[1], gain_rest[1], hm, hr, 2 * at, 2 * at + 1, at)

        for part in parts:
            own_copy(step, part).wait_recv()
            inner_copy(step, part).start()

            @pl.when(has_across)
            def _(step=step, part=part):
                across_copy(step, part).start()

            begin, size = PARTS[part]
            spot = slice(begin, begin + size)
            norm_pair(own[spot], gain_main[0], gain_rest[0], xm, xr, 2, 3, 1, spot)
        for tile in range(4):
            part = after_part(xm, 2, xr[1], wm.at[0], w_own.at[0], we.at[0], e_own.at[0], tile)
            if tile == 3:
                zfe[...] = part
            else:
                zf[:, columns(tile)] = part

        for part in parts:
            inner_copy(step, part).wait_recv()
        norm_pair(near[...], gain_main[0], gain_rest[0], xm, xr, 5, 4, 2)
        rests = jnp.concatenate([xr[1], xr[2]], axis=1)
        own_turned = roll_rest(rests_of(own))
        centre = (second_of(own), second_of(near), jnp.where(low, own_turned, rests_of(near)))
        products = [both_parts(xm, 2, rests, wm.at[0], w_near, we.at[0], e_near, tile) for tile in range(4)]
        results = finish(
            lambda tile, row: products[tile] if row is None else products[tile][row * PIX : (row + 1) * PIX],
            centre, wt[0], bias_main[0], bias_rest[0],
        )
        keep(1, *results)
        for tile in range(4):
            part = after_part(hm, 2, hr[1], wm.at[1], w_own.at[1], we.at[1], e_own.at[1], tile)
            if tile == 3:
                zhe[...] = part
            else:
                zh[:, columns(tile)] = part

        def early(z, ends, tile, row):
            return ends[...] if row is None else z[row * PIX : (row + 1) * PIX, columns(tile)]

        @pl.when(has_across)
        def _(step=step):
            for part in parts:
                across_copy(step, part).wait_recv()

        norm_pair(far[...], gain_main[0], gain_rest[0], xm, xr, 1, 0, 0)
        centre = (first_of(far), first_of(own), jnp.where(low, rests_of(far), own_turned))
        main_a, main_b, rest = finish(
            lambda tile, row: early(zf, zfe, tile, row) + before_part(xm, 0, xr[0], wm.at[0], w_far, we.at[0], e_far, tile, row),
            centre, wt[0], bias_main[0], bias_rest[0],
        )
        keep(0, jnp.where(has_across, main_a, 0.0), main_b, jnp.where(low, jnp.where(has_across, rest, 0.0), rest))
        centre = (
            second_of(hidden.at[0]),
            first_of(hidden.at[1]),
            roll_rest(jnp.where(low, rests_of(hidden.at[1]), rests_of(hidden.at[0]))),
        )
        main_a, main_b, rest = finish(
            lambda tile, row: early(zh, zhe, tile, row) + before_part(hm, 0, hr[0], wm.at[1], w_hid, we.at[1], e_hid, tile, row),
            centre, wt[1], bias_main[1], bias_rest[1],
        )
        main_a = jnp.where(two_main, main_a, centre[0])
        main_b = jnp.where(two_main, main_b, centre[1])
        rest = jnp.where(two, rest, centre[2])
        if step + 1 < STEPS:
            packed[step + 1] = jnp.concatenate([main_a, main_b, rest], axis=1).astype(BF16)
            send(step + 1)
        else:
            out[...] = jnp.concatenate([main_a, main_b, rest], axis=1).astype(BF16)

    for step in range(STEPS):
        for part in parts:
            inner_copy(step, part).wait_send()
            if part >= 1:
                own_copy(step, part).wait_send()

        @pl.when(jnp.logical_not(goes_first))
        def _(step=step):
            for part in range(1):
                own_copy(step, part).wait_send()

        @pl.when(has_across)
        def _(step=step):
            for part in parts:
                across_copy(step, part).wait_send()


def unpack(pair, out, strip, pixels):
    core = lax.rem(lax.axis_index("rows"), 2)
    low_half = lanes((W // 2, 128)) < REST
    rest = rests_of(pair)
    for at, (main, ends) in enumerate(((first_of(pair), rest), (second_of(pair), roll_rest(rest)))):
        pixels[at, 0], pixels[at, 1], pixels[at, 2] = main[:, :128], main[:, 128:], ends
    for f in range(FRAMES):
        for row, at in ((0, core), (1, 1 - core)):
            even, odd = (
                [pixels[at, k, pl.ds(f * W + one, W // 2, stride=2)] for k in range(3)] for one in range(2)
            )
            odd = [roll_rest(tile) for tile in odd]
            own = [even[0], even[1]]
            own += [jnp.where(low_half, one, two) for one, two in ((even[2], odd[0]), odd[:2], odd[1:])]
            for k in range(TILES):
                strip[f, k, pl.ds(row, W // 2, stride=2)] = own[k]
        for pair in range(W // 2):
            for k in range(TILES):
                begin = 2 * C * pair + 128 * k
                out[0, f, :, begin : begin + 128] = strip[f, k, 2 * pair : 2 * pair + 2].astype(BF16)


def body(state, bounds, timesteps, gains, spatial_weight, temporal_weight, time_weight):
    vmem = pl.BlockSpec(memory_space=pltpu.VMEM)
    smem = pl.BlockSpec(memory_space=pltpu.SMEM)
    hbm = pl.BlockSpec(memory_space=pl.ANY)
    pair = pl.pallas_call(
        kernel,
        out_shape=pltpu.VMEM((PIX, PACK), BF16),
        in_specs=[hbm, smem, smem, vmem, hbm, hbm, hbm],
        out_specs=vmem,
        scratch_shapes=[
            pltpu.VMEM((FRAMES, 2, W * C), BF16),
            pltpu.VMEM((FRAMES, TILES, W, 128), F32),
            pltpu.VMEM((2, 3, PIX, 128), F32),
            pltpu.VMEM((2, 9, C, C), BF16),
            pltpu.VMEM((2, 3, C, C), BF16),
            pltpu.VMEM((2, C, C), F32),
            pltpu.VMEM((2, 3 * MAIN, NOUT), BF16),
            pltpu.VMEM((2, 4 * REST, NOUT), BF16),
            pltpu.VMEM((2, 2, 2 * REST, NOUT), BF16),
            pltpu.VMEM((2, 2 * REST, NOUT), BF16),
            pltpu.VMEM((2, 2 * REST, NOUT), BF16),
            pltpu.VMEM((2, 4 * MAIN, NENDS), BF16),
            pltpu.VMEM((4 * REST, NENDS), BF16),
            pltpu.VMEM((2, 2 * REST, NENDS), BF16),
            pltpu.VMEM((2 * REST, NENDS), BF16),
            pltpu.VMEM((2 * REST, NENDS), BF16),
            pltpu.VMEM((2, 2 * MAIN, 2 * MAIN), BF16),
            pltpu.VMEM((2, 2, 4 * REST, 2 * MAIN), BF16),
            pltpu.VMEM((2, 4 * MAIN + 4 * REST, 4 * REST), BF16),
            pltpu.VMEM((STEPS, PIX, PACK), BF16),
            pltpu.VMEM((STEPS, 3, PIX, PACK), BF16),
            pltpu.VMEM((2, PIX, PACK), BF16),
            pltpu.VMEM((6, PIX, MAIN), BF16),
            pltpu.VMEM((3, PIX, 128), BF16),
            pltpu.VMEM((4, PIX, MAIN), BF16),
            pltpu.VMEM((2, PIX, 128), BF16),
            pltpu.VMEM((2 * PIX, NOUT), F32),
            pltpu.VMEM((2 * PIX, NOUT), F32),
            pltpu.VMEM((PIX, NENDS), F32),
            pltpu.VMEM((PIX, NENDS), F32),
            pltpu.SemaphoreType.DMA((3, 3)),
            pltpu.SemaphoreType.DMA((STEPS, 3, len(PARTS))),
            pltpu.SemaphoreType.DMA((STEPS, 3, len(PARTS))),
            pltpu.SemaphoreType.REGULAR((STEPS,)),
        ],
        compiler_params=pltpu.CompilerParams(
            collective_id=1, has_side_effects=True, vmem_limit_bytes=56 << 20
        ),
        cost_estimate=pl.CostEstimate(flops=4 << 30, bytes_accessed=6 << 20, transcendentals=1 << 20),
        name="cycle",
    )(
        state,
        bounds,
        timesteps,
        gains.reshape(2, C),
        spatial_weight.reshape(2, 9, C, C),
        temporal_weight.reshape(2, 3, C, C),
        time_weight.reshape(2, C, C),
    )
    return pl.pallas_call(
        unpack,
        out_shape=jax.ShapeDtypeStruct((1, FRAMES, 2, W * C), BF16),
        in_specs=[vmem],
        out_specs=vmem,
        scratch_shapes=[pltpu.VMEM((FRAMES, TILES, W, 128), F32), pltpu.VMEM((2, 3, PIX, 128), F32)],
        compiler_params=pltpu.CompilerParams(vmem_limit_bytes=16 << 20),
        name="unpack",
    )(pair)


def solution(mesh):
    placed = (
        P("segment", None, "rows", None),
        P(),
        P(),
        P("segment", None, None),
        P("segment", None, None, None, None, None),
        P("segment", None, None, None, None),
        P("segment", None, None, None),
    )
    return jax.shard_map(
        body,
        mesh=mesh,
        in_specs=placed,
        out_specs=P("segment", None, "rows", None),
        check_vma=False,
    )
```

```python
import math

import jax
import jax.numpy as jnp
from jax import lax
from jax.experimental import pallas as pl
from jax.experimental.pallas import tpu as pltpu
from jax.sharding import PartitionSpec as P

C = 320
W = 72
STEPS = 2
CHAIN = 8
FRAMES = 2
SEGMENTS = 4
GROUPS = 64
MAIN = 256
REST = C - MAIN
PIX = FRAMES * W
PACK = 2 * MAIN + 2 * REST
TILES = 2 * C // 128
NOUT = 3 * MAIN
NENDS = 3 * 128
PARTS = ((0, 32), (32, 32), (64, 32), (96, 32), (128, 16))
NEAR = ((0, 1, None, 2), (None, 0, 2, 1))
AFTER = ((2, None), (1, 2))
BEFORE = ((0, 1), (None, 0))
BEFORE_REVERSED = ((1, 0), (0, None))
MESH = pl.DeviceIdType.MESH
F32 = jnp.float32
BF16 = jnp.bfloat16


def lanes(shape):
    return lax.broadcasted_iota(jnp.int32, shape, len(shape) - 1)


def roll_rest(value):
    return pltpu.roll(value, REST, 1)


def norm_pair(pair, gain_main, gain_rest, xm, xr, first, second, at, spot=slice(None)):
    main_a = pair[:, :MAIN].astype(F32)
    main_b = pair[:, MAIN : 2 * MAIN].astype(F32)
    rest = pair[:, 2 * MAIN :].astype(F32)
    low = lanes(rest.shape) < REST
    square = rest * rest
    zero = jnp.zeros_like(square)

    def scale(main, own):
        both = main * main
        total = both[:, :128] + both[:, 128:] + own
        return lax.rsqrt(jnp.sum(total, axis=-1, keepdims=True) * (1.0 / C) + 1e-06)

    scale_a = scale(main_a, jnp.where(low, square, zero))
    scale_b = scale(main_b, jnp.where(low, zero, square))
    xm[first, spot] = (main_a * scale_a * gain_main).astype(BF16)
    xm[second, spot] = (main_b * scale_b * gain_main).astype(BF16)
    xr[at, spot] = (rest * jnp.where(low, scale_a, scale_b) * gain_rest).astype(BF16)


def first_of(pair):
    return pair[:, :MAIN].astype(F32)


def second_of(pair):
    return pair[:, MAIN : 2 * MAIN].astype(F32)


def rests_of(pair):
    return pair[:, 2 * MAIN :].astype(F32)


def dot(left, right):
    return jnp.dot(left, right, preferred_element_type=F32)


def columns(tile):
    return slice(tile * MAIN, (tile + 1) * MAIN)


def before_part(xm, row, rest, wm, wr, we, we_rest, tile, out_row):
    cols = columns(tile)
    both = jnp.concatenate([xm[row], xm[row + 1]], axis=1)
    if tile == 3:
        return dot(both, we[: 2 * MAIN]) + dot(rest, we_rest[...])
    if out_row == 0:
        return dot(both, wm[: 2 * MAIN, cols]) + dot(rest, wr[0, :, cols])
    return dot(xm[row + 1], wm[:MAIN, cols]) + dot(rest, wr[1, :, cols])


def after_part(xm, row, rest, wm, wr, we, we_rest, tile):
    cols = columns(tile)
    both = jnp.concatenate([xm[row], xm[row + 1]], axis=1)
    if tile == 3:
        return dot(both, we[2 * MAIN :]) + dot(rest, we_rest[...])
    one = dot(xm[row], wm[2 * MAIN :, cols]) + dot(rest, wr[0, :, cols])
    two = dot(both, wm[MAIN:, cols]) + dot(rest, wr[1, :, cols])
    return jnp.concatenate([one, two], axis=0)


def both_parts(xm, row, rest, wm, wr, we, we_rest, tile):
    cols = columns(tile)
    if tile == 3:
        return dot(jnp.concatenate([xm[row + at] for at in range(4)], axis=1), we[...]) + dot(rest, we_rest[...])
    left = jnp.concatenate([xm[row + dy : row + dy + 2].reshape(2 * PIX, MAIN) for dy in range(3)], axis=1)
    rests = jnp.concatenate([dot(rest, wr[0, :, cols]), dot(rest, wr[1, :, cols])], axis=0)
    return dot(left, wm[:, cols]) + rests


def finish(product, centre, wt, bias_main, bias_rest):
    wt_main, wt_rest, wt_ends = wt

    def from_before(value):
        spot = lax.rem(lax.broadcasted_iota(jnp.int32, (value.shape[0], 1), 0), W)
        return jnp.where(spot == 0, 0.0, pltpu.roll(value, 1, 0))

    def from_after(value):
        spot = lax.rem(lax.broadcasted_iota(jnp.int32, (value.shape[0], 1), 0), W)
        return jnp.where(spot == W - 1, 0.0, pltpu.roll(value, value.shape[0] - 1, 0))

    def silu(value):
        return value * (0.5 * jnp.tanh(0.5 * value) + 0.5)

    z = product(3, None)
    a_rest = from_before(z[:, :128]) + z[:, 128:256] + from_after(z[:, 256:]) + bias_rest
    u_rest = silu(a_rest)
    a_main, lines = [], []
    for row in range(2):
        taps = [product(tile, row) for tile in range(3)]
        a_main.append(from_before(taps[0]) + taps[1] + from_after(taps[2]) + bias_main)
        u_main = silu(a_main[row])
        lines.append([u_main[:W], u_main[W:]])
    mixed = jnp.concatenate([jnp.concatenate([lines[row][f] for row in range(2)], axis=0) for f in range(FRAMES)], axis=1)
    mixed = mixed.astype(BF16)
    ends = jnp.concatenate([u_rest[:W], u_rest[W:]], axis=1).astype(BF16)
    wide = jnp.concatenate([lines[row][f] for row in range(2) for f in range(FRAMES)], axis=1).astype(BF16)
    v_rest = dot(wide, wt_ends[: 4 * MAIN]) + dot(ends, wt_ends[4 * MAIN :])
    v = dot(mixed, wt_main[...])
    v_rows = []
    for row in range(2):
        own = v[row * W : (row + 1) * W] + dot(ends, wt_rest[row])
        v_rows.append(jnp.concatenate([own[:, :MAIN], own[:, MAIN:]], axis=0))
    v_rest = jnp.concatenate([v_rest[:, :128], v_rest[:, 128:]], axis=0)
    h_a, h_b, h_rest = centre
    return h_a + a_main[0] + v_rows[0], h_b + a_main[1] + v_rows[1], h_rest + a_rest + v_rest


def kernel(
    state, bounds, timesteps, gains, spatial, temporal, time_weight,
    out,
    raw_x, strip, pixels, raw_s, raw_t, raw_b, wm, w_near, w_own, w_far, w_hid, we, e_near, e_own, e_far, e_hid, wt_main, wt_rest, wt_ends,
    packed, arrived, hidden, xm, xr, hm, hr, zf, zh, zfe, zhe,
    load_sem, send_sem, recv_sem, go_sem,
):
    segment = lax.axis_index("segment")
    group = lax.axis_index("rows")
    core = lax.rem(group, 2)
    behind, ahead = lax.rem(segment + SEGMENTS - 1, SEGMENTS), lax.rem(segment + 1, SEGMENTS)
    across = group - 1 + 2 * core
    inner = group + 1 - 2 * core
    has_across = (across >= 0) & (across < GROUPS)
    edge = lax.rem(group, CHAIN)
    leader = jnp.where(edge < 2, 0, 1)
    goes_first = core == leader
    goes_after = core != leader

    loads = []
    for slot in range(2):
        loads.append(
            (
                pltpu.make_async_copy(spatial.at[slot], raw_s.at[slot], load_sem.at[slot, 0]),
                pltpu.make_async_copy(temporal.at[slot], raw_t.at[slot], load_sem.at[slot, 1]),
                pltpu.make_async_copy(time_weight.at[slot], raw_b.at[slot], load_sem.at[slot, 2]),
            )
        )

    barrier = pltpu.get_barrier_semaphore()
    pl.semaphore_signal(barrier, inc=1, device_id=(behind, group), device_id_type=MESH)
    pl.semaphore_signal(barrier, inc=1, device_id=(segment, inner), device_id_type=MESH)

    @pl.when(has_across)
    def _():
        pl.semaphore_signal(barrier, inc=1, device_id=(segment, across), device_id_type=MESH)

    state_load = pltpu.make_async_copy(state.at[0], raw_x, load_sem.at[2, 0])
    for load in (state_load, *loads[0], *loads[1]):
        load.start()

    state_load.wait()
    low_half = lanes((W // 2, 128)) < REST
    for f in range(FRAMES):
        for pair in range(W // 2):
            for k in range(TILES):
                begin = 2 * C * pair + 128 * k
                strip[f, k, 2 * pair : 2 * pair + 2] = raw_x[f, :, begin : begin + 128].astype(F32)
        for row, at in ((0, core), (1, 1 - core)):
            own = [strip[f, k, pl.ds(row, W // 2, stride=2)] for k in range(TILES)]
            swapped = [None, None] + [roll_rest(tile) for tile in own[2:]]
            odd = [jnp.where(low_half, swapped[2 + k], swapped[min(3 + k, 4)]) for k in range(3)]
            for k in range(3):
                pixels[at, k, pl.ds(f * W, W // 2, stride=2)] = own[k]
                pixels[at, k, pl.ds(f * W + 1, W // 2, stride=2)] = odd[k]
    rest = jnp.where(lanes((PIX, 128)) < REST, pixels[0, 2], roll_rest(pixels[1, 2]))
    packed[0] = jnp.concatenate([pixels[at, k] for at in range(2) for k in range(2)] + [rest], axis=1).astype(BF16)

    pl.semaphore_wait(barrier, 2 + has_across.astype(jnp.int32))

    def piece(step, kind, part, source, target, device):
        spot = pl.ds(*PARTS[part])
        return pltpu.make_async_remote_copy(
            source.at[spot], target.at[spot], send_sem.at[step, kind, part], recv_sem.at[step, kind, part],
            device_id=device, device_id_type=MESH,
        )

    def own_copy(step, part):
        return piece(step, 0, part, packed.at[step], arrived.at[step, 1], (ahead, group))

    def across_copy(step, part):
        return piece(step, 1, part, arrived.at[step, 1], arrived.at[step, 0], (segment, across))

    def inner_copy(step, part):
        return piece(step, 2, part, arrived.at[step, 1], arrived.at[step, 2], (segment, inner))

    parts = range(len(PARTS))

    def send(step):
        @pl.when(goes_after)
        def _():
            pl.semaphore_wait(go_sem.at[step], 1)

        for part in parts:
            own_copy(step, part).start()

        @pl.when(goes_first)
        def _():
            for part in range(1):
                own_copy(step, part).wait_send()
            pl.semaphore_signal(go_sem.at[step], inc=1, device_id=(segment, inner), device_id_type=MESH)

    send(0)

    @pl.when(jnp.logical_not(has_across))
    def _():
        for step in range(STEPS):
            arrived[step, 0] = jnp.zeros((PIX, PACK), BF16)

    none = jnp.zeros((REST, NOUT), BF16)
    wt = [(wt_main.at[slot], wt_rest.at[slot], wt_ends.at[slot]) for slot in range(2)]
    for slot in range(2):
        for load in loads[slot]:
            load.wait()
        for dy in range(3):
            taps = [3 * (dy + core * (2 - 2 * dy)) + dx for dx in range(3)]
            for dx in range(3):
                wm[slot, dy * MAIN : (dy + 1) * MAIN, columns(dx)] = raw_s[slot, taps[dx], :MAIN, :MAIN]
            tail = jnp.concatenate([raw_s[slot, tap, MAIN:, :MAIN] for tap in taps], axis=1)
            if slot == 0:
                places = ((w_near, NEAR), (w_own.at[slot], AFTER), (w_far, BEFORE_REVERSED))
            else:
                places = ((w_own.at[slot], AFTER), (w_hid, BEFORE))
            for ref, order in places:
                for row in range(2):
                    for at, tap in enumerate(order[row]):
                        if tap == dy:
                            ref[row, at * REST : (at + 1) * REST] = tail
                        elif tap is None and dy == 0:
                            ref[row, at * REST : (at + 1) * REST] = none
        blank = jnp.zeros((C, REST), BF16)

        def ends_of(i):
            tap = lambda dy, dx: raw_s[slot, 3 * (dy + core * (2 - 2 * dy)) + dx, :, MAIN:] if 0 <= dy < 3 else blank
            return jnp.concatenate([tap(i - row, dx) for dx in range(3) for row in range(2)], axis=1)

        ends = [ends_of(i) for i in range(4)]
        for i in range(4):
            we[slot, i * MAIN : (i + 1) * MAIN] = ends[i][:MAIN]
        places = ((e_near, (0, 1, 3, 2)), (e_own.at[slot], (2, 3)), (e_far, (1, 0)))
        for ref, order in places if slot == 0 else ((e_own.at[slot], (2, 3)), (e_hid, (0, 1))):
            for at, i in enumerate(order):
                ref[at * REST : (at + 1) * REST] = ends[i][MAIN:]
        nil = jnp.zeros((REST, FRAMES * MAIN), BF16)
        blank = jnp.zeros((C, REST), BF16)
        for f in range(FRAMES):
            taps = [f - g + 1 for g in range(FRAMES)]
            for g in range(FRAMES):
                wt_main[slot, f * MAIN : (f + 1) * MAIN, columns(g)] = raw_t[slot, taps[g], :MAIN, :MAIN]
            tail = jnp.concatenate([raw_t[slot, tap, MAIN:, :MAIN] for tap in taps], axis=1)
            for row in range(2):
                for at in range(2):
                    begin = (2 * f + at) * REST
                    wt_rest[slot, row, begin : begin + REST] = tail if at == row else nil
                ends = [raw_t[slot, tap, :, MAIN:] for tap in taps]
                ends = jnp.concatenate([ends[g] if at == row else blank for g in range(FRAMES) for at in range(2)], axis=1)
                wt_ends[slot, (2 * row + f) * MAIN : (2 * row + f + 1) * MAIN] = ends[:MAIN]
                begin = 4 * MAIN + (2 * f + row) * REST
                wt_ends[slot, begin : begin + REST] = ends[MAIN:]

    half = C // 2
    number = lax.broadcasted_iota(jnp.int32, (8, half), 1).astype(F32)
    which = lax.broadcasted_iota(jnp.int32, (8, half), 0)
    t = jnp.where(which == 0, timesteps[0], timesteps[1]).astype(F32)
    angle = t * jnp.exp(-math.log(10000.0) * number / half)
    emb = jnp.concatenate([jnp.cos(angle), jnp.sin(angle)], axis=1)
    bias = [
        jnp.dot(emb, raw_b[slot], preferred_element_type=F32, precision=lax.Precision.HIGHEST) for slot in range(2)
    ]

    def twice(value):
        return jnp.concatenate([value, value], axis=1)

    gain_main = [gains[slot : slot + 1, :MAIN] for slot in range(2)]
    gain_rest = [twice(gains[slot : slot + 1, MAIN:]) for slot in range(2)]
    two = jnp.full((1, 128), bounds[segment + 1] - bounds[segment], jnp.int32) > 1
    two_main = jnp.concatenate([two, two], axis=1)
    low = lanes((PIX, 128)) < REST

    for step in range(STEPS):
        bias_main = [bias[slot][step : step + 1, :MAIN] for slot in range(2)]
        bias_rest = [twice(bias[slot][step : step + 1, MAIN:]) for slot in range(2)]
        far, own, near = (arrived.at[step, at] for at in range(3))

        def keep(at, main_a, main_b, rest):
            hidden[at] = jnp.concatenate([main_a, main_b, rest], axis=1).astype(BF16)
            norm_pair(hidden[at], gain_main[1], gain_rest[1], hm, hr, 2 * at, 2 * at + 1, at)

        for part in parts:
            own_copy(step, part).wait_recv()
            inner_copy(step, part).start()

            @pl.when(has_across)
            def _(step=step, part=part):
                across_copy(step, part).start()

            begin, size = PARTS[part]
            spot = slice(begin, begin + size)
            norm_pair(own[spot], gain_main[0], gain_rest[0], xm, xr, 2, 3, 1, spot)
        for tile in range(4):
            part = after_part(xm, 2, xr[1], wm.at[0], w_own.at[0], we.at[0], e_own.at[0], tile)
            if tile == 3:
                zfe[...] = part
            else:
                zf[:, columns(tile)] = part

        for part in parts:
            inner_copy(step, part).wait_recv()
        norm_pair(near[...], gain_main[0], gain_rest[0], xm, xr, 5, 4, 2)
        rests = jnp.concatenate([xr[1], xr[2]], axis=1)
        own_turned = roll_rest(rests_of(own))
        centre = (second_of(own), second_of(near), jnp.where(low, own_turned, rests_of(near)))
        products = [both_parts(xm, 2, rests, wm.at[0], w_near, we.at[0], e_near, tile) for tile in range(4)]
        results = finish(
            lambda tile, row: products[tile] if row is None else products[tile][row * PIX : (row + 1) * PIX],
            centre, wt[0], bias_main[0], bias_rest[0],
        )
        keep(1, *results)
        for tile in range(4):
            part = after_part(hm, 2, hr[1], wm.at[1], w_own.at[1], we.at[1], e_own.at[1], tile)
            if tile == 3:
                zhe[...] = part
            else:
                zh[:, columns(tile)] = part

        def early(z, ends, tile, row):
            return ends[...] if row is None else z[row * PIX : (row + 1) * PIX, columns(tile)]

        @pl.when(has_across)
        def _(step=step):
            for part in parts:
                across_copy(step, part).wait_recv()

        norm_pair(far[...], gain_main[0], gain_rest[0], xm, xr, 1, 0, 0)
        centre = (first_of(far), first_of(own), jnp.where(low, rests_of(far), own_turned))
        main_a, main_b, rest = finish(
            lambda tile, row: early(zf, zfe, tile, row) + before_part(xm, 0, xr[0], wm.at[0], w_far, we.at[0], e_far, tile, row),
            centre, wt[0], bias_main[0], bias_rest[0],
        )
        keep(0, jnp.where(has_across, main_a, 0.0), main_b, jnp.where(low, jnp.where(has_across, rest, 0.0), rest))
        centre = (
            second_of(hidden.at[0]),
            first_of(hidden.at[1]),
            roll_rest(jnp.where(low, rests_of(hidden.at[1]), rests_of(hidden.at[0]))),
        )
        main_a, main_b, rest = finish(
            lambda tile, row: early(zh, zhe, tile, row) + before_part(hm, 0, hr[0], wm.at[1], w_hid, we.at[1], e_hid, tile, row),
            centre, wt[1], bias_main[1], bias_rest[1],
        )
        main_a = jnp.where(two_main, main_a, centre[0])
        main_b = jnp.where(two_main, main_b, centre[1])
        rest = jnp.where(two, rest, centre[2])
        if step + 1 < STEPS:
            packed[step + 1] = jnp.concatenate([main_a, main_b, rest], axis=1).astype(BF16)
            send(step + 1)
        else:
            out[...] = jnp.concatenate([main_a, main_b, rest], axis=1).astype(BF16)

    for step in range(STEPS):
        for part in parts:
            inner_copy(step, part).wait_send()
            if part >= 1:
                own_copy(step, part).wait_send()

        @pl.when(jnp.logical_not(goes_first))
        def _(step=step):
            for part in range(1):
                own_copy(step, part).wait_send()

        @pl.when(has_across)
        def _(step=step):
            for part in parts:
                across_copy(step, part).wait_send()


def unpack(pair, out, strip, pixels):
    core = lax.rem(lax.axis_index("rows"), 2)
    low_half = lanes((W // 2, 128)) < REST
    rest = rests_of(pair)
    for at, (main, ends) in enumerate(((first_of(pair), rest), (second_of(pair), roll_rest(rest)))):
        pixels[at, 0], pixels[at, 1], pixels[at, 2] = main[:, :128], main[:, 128:], ends
    for f in range(FRAMES):
        for row, at in ((0, core), (1, 1 - core)):
            even, odd = (
                [pixels[at, k, pl.ds(f * W + one, W // 2, stride=2)] for k in range(3)] for one in range(2)
            )
            odd = [roll_rest(tile) for tile in odd]
            own = [even[0], even[1]]
            own += [jnp.where(low_half, one, two) for one, two in ((even[2], odd[0]), odd[:2], odd[1:])]
            for k in range(TILES):
                strip[f, k, pl.ds(row, W // 2, stride=2)] = own[k]
        for pair in range(W // 2):
            for k in range(TILES):
                begin = 2 * C * pair + 128 * k
                out[0, f, :, begin : begin + 128] = strip[f, k, 2 * pair : 2 * pair + 2].astype(BF16)


def body(state, bounds, timesteps, gains, spatial_weight, temporal_weight, time_weight):
    vmem = pl.BlockSpec(memory_space=pltpu.VMEM)
    smem = pl.BlockSpec(memory_space=pltpu.SMEM)
    hbm = pl.BlockSpec(memory_space=pl.ANY)
    pair = pl.pallas_call(
        kernel,
        out_shape=pltpu.VMEM((PIX, PACK), BF16),
        in_specs=[hbm, smem, smem, vmem, hbm, hbm, hbm],
        out_specs=vmem,
        scratch_shapes=[
            pltpu.VMEM((FRAMES, 2, W * C), BF16),
            pltpu.VMEM((FRAMES, TILES, W, 128), F32),
            pltpu.VMEM((2, 3, PIX, 128), F32),
            pltpu.VMEM((2, 9, C, C), BF16),
            pltpu.VMEM((2, 3, C, C), BF16),
            pltpu.VMEM((2, C, C), F32),
            pltpu.VMEM((2, 3 * MAIN, NOUT), BF16),
            pltpu.VMEM((2, 4 * REST, NOUT), BF16),
            pltpu.VMEM((2, 2, 2 * REST, NOUT), BF16),
            pltpu.VMEM((2, 2 * REST, NOUT), BF16),
            pltpu.VMEM((2, 2 * REST, NOUT), BF16),
            pltpu.VMEM((2, 4 * MAIN, NENDS), BF16),
            pltpu.VMEM((4 * REST, NENDS), BF16),
            pltpu.VMEM((2, 2 * REST, NENDS), BF16),
            pltpu.VMEM((2 * REST, NENDS), BF16),
            pltpu.VMEM((2 * REST, NENDS), BF16),
            pltpu.VMEM((2, 2 * MAIN, 2 * MAIN), BF16),
            pltpu.VMEM((2, 2, 4 * REST, 2 * MAIN), BF16),
            pltpu.VMEM((2, 4 * MAIN + 4 * REST, 4 * REST), BF16),
            pltpu.VMEM((STEPS, PIX, PACK), BF16),
            pltpu.VMEM((STEPS, 3, PIX, PACK), BF16),
            pltpu.VMEM((2, PIX, PACK), BF16),
            pltpu.VMEM((6, PIX, MAIN), BF16),
            pltpu.VMEM((3, PIX, 128), BF16),
            pltpu.VMEM((4, PIX, MAIN), BF16),
            pltpu.VMEM((2, PIX, 128), BF16),
            pltpu.VMEM((2 * PIX, NOUT), F32),
            pltpu.VMEM((2 * PIX, NOUT), F32),
            pltpu.VMEM((PIX, NENDS), F32),
            pltpu.VMEM((PIX, NENDS), F32),
            pltpu.SemaphoreType.DMA((3, 3)),
            pltpu.SemaphoreType.DMA((STEPS, 3, len(PARTS))),
            pltpu.SemaphoreType.DMA((STEPS, 3, len(PARTS))),
            pltpu.SemaphoreType.REGULAR((STEPS,)),
        ],
        compiler_params=pltpu.CompilerParams(
            collective_id=1, has_side_effects=True, vmem_limit_bytes=56 << 20
        ),
        cost_estimate=pl.CostEstimate(flops=4 << 30, bytes_accessed=6 << 20, transcendentals=1 << 20),
        name="cycle",
    )(
        state,
        bounds,
        timesteps,
        gains.reshape(2, C),
        spatial_weight.reshape(2, 9, C, C),
        temporal_weight.reshape(2, 3, C, C),
        time_weight.reshape(2, C, C),
    )
    return pl.pallas_call(
        unpack,
        out_shape=jax.ShapeDtypeStruct((1, FRAMES, 2, W * C), BF16),
        in_specs=[vmem],
        out_specs=vmem,
        scratch_shapes=[pltpu.VMEM((FRAMES, TILES, W, 128), F32), pltpu.VMEM((2, 3, PIX, 128), F32)],
        compiler_params=pltpu.CompilerParams(vmem_limit_bytes=16 << 20),
        name="unpack",
    )(pair)


def solution(mesh):
    placed = (
        P("segment", None, "rows", None),
        P(),
        P(),
        P("segment", None, None),
        P("segment", None, None, None, None, None),
        P("segment", None, None, None, None),
        P("segment", None, None, None),
    )
    return jax.shard_map(
        body,
        mesh=mesh,
        in_specs=placed,
        out_specs=P("segment", None, "rows", None),
        check_vma=False,
    )
```
